256 devices in a mesh: head: 8 (over x, y_hi), seq: 32 (over y_lo, z, core).
Axes of the slice: x: 4, y: 4 (y_hi: 2, y_lo: 2; y = y_hi * 2 + y_lo), z: 8, core: 2. Of those that a mesh axis runs over, the one named last changes fastest.
Arguments:
- video_q: bfloat16 [8192, 3072], P(('seq', 'head')), may hold values from -160 to 160
- video_k: bfloat16 [8192, 3072], P(('seq', 'head')), may hold values from -6 to 6
- video_v: bfloat16 [8192, 3072], P(('seq', 'head')), may hold values from -6 to 6
- audio_q: bfloat16 [512, 3072], P('seq', 'head'), may hold values from -160 to 160
- audio_k: bfloat16 [512, 3072], P('seq', 'head'), may hold values from -6 to 6
- audio_v: bfloat16 [512, 3072], P('seq', 'head'), may hold values from -6 to 6
- align: int32 [8192], P(('seq', 'head')), may hold values from 0 to 511, as said below
Outputs:
- video_out: bfloat16 [8192, 3072], P(('seq', 'head'))
- audio_out: bfloat16 [512, 3072], P('seq', 'head')
The draws below stay inside these ranges and needn't reach their ends.
Inputs may be any that keep to these rules, and one draw needn't show every extreme that they name: align is non-decreasing, align[0] = 0, align[8191] = 511, and every align[i] lies within 2 of floor(i * 512 / 8192).
All inputs are finite; a program needn't handle non-finite values.
Results may differ from the reference program's by a relative error of at most 0.025.
Values may be sent and summed in bfloat16 or wider, within the bound.
No kernel may reach another device: no remote copies, remote signals or barrier semaphores. Data moves between devices by JAX's collectives and lax.ppermute only.
A program may use at most 128 MiB of HBM per device.

```python
import jax
import jax.numpy as jnp
from jax import lax

HEADS = 24
HD = 128
D = 3072
A_DEV = 16
VT = 8192
AT = 512
WIN = 64
N_SEQ = 32


def planted(key, salt, count, strength_on):
    key = jax.random.fold_in(key, salt)
    key_q, key_k, key_t, key_s = jax.random.split(key, 4)
    keys = jnp.clip(jax.random.normal(key_k, (count, D), jnp.float32), -6.0, 6.0)
    queries = jnp.clip(jax.random.normal(key_q, (count, D), jnp.float32), -6.0, 6.0)
    picks = count // 64
    rows = jnp.arange(picks, dtype=jnp.int32) * 64
    target = jax.random.randint(key_t, (picks,), 0, count - 1)
    strength = jax.random.uniform(key_s, (picks, 1), jnp.float32, 9.0, 25.0)
    near = jnp.where(strength_on > 0.0, 0.99 * keys[target], keys[target + 1])
    keys = keys.at[target + 1].set(near)
    lifted = jnp.where(strength_on > 0.0, strength * keys[target], queries[rows])
    queries = queries.at[rows].set(lifted)
    return (queries, keys)


def draw_video_q(key, part):
    return planted(key, 11, VT, 0.0)[0].astype(jnp.bfloat16)


def draw_video_k(key, part):
    return planted(key, 11, VT, 0.0)[1].astype(jnp.bfloat16)


def draw_audio_q(key, part):
    return planted(key, 23, AT, 0.0)[0].astype(jnp.bfloat16)


def draw_audio_k(key, part):
    return planted(key, 23, AT, 0.0)[1].astype(jnp.bfloat16)


def draw_align(key, part):
    key = jax.random.fold_in(key, 37)
    nominal = jnp.arange(VT, dtype=jnp.int32) * AT // VT
    jitter = jax.random.randint(key, (VT,), -2, 3)
    stamps = jnp.clip(nominal + jitter, 0, AT - 1).astype(jnp.int32)
    stamps = stamps.at[0].set(0)
    stamps = lax.cummax(stamps, axis=0)
    stamps = stamps.at[VT - 1].set(AT - 1)
    return stamps.astype(jnp.int32)


def levels(rng, dims, pieces, smallest, high):
    def one(axis_at, shards_of):
        draws = jax.random.uniform(jax.random.fold_in(jax.random.fold_in(rng, 6), axis_at), (shards_of,), jnp.float32, smallest / len(pieces), high / len(pieces))
        return jnp.repeat(jnp.exp(draws), dims[axis_at] // shards_of).reshape((-1,) + (1,) * (len(dims) - axis_at - 1))

    factor_of = one(*pieces[0])
    for cut in pieces[1:]:
        factor_of = factor_of * one(*cut)
    return factor_of


def noise(rng, shape, spread, most, pieces=(), held_as=jnp.bfloat16):
    loudness = levels(rng, shape, pieces, -0.22, 0.18) if pieces else 1.0
    result = jax.random.normal(rng, shape, jnp.float32) * spread * loudness
    return jnp.minimum(jnp.maximum(result, -most), most).astype(held_as)


def setup_inputs(seed: int = 0) -> dict:
    key_list = jax.random.split(jax.random.key(seed), 8)
    return {
        "video_q": draw_video_q(jax.random.fold_in(key_list[7], 71), 0),
        "video_k": draw_video_k(jax.random.fold_in(key_list[7], 71), 0),
        "video_v": noise(key_list[2], (VT, D), 1.0, 6.0, ((0, 256),)),
        "audio_q": draw_audio_q(jax.random.fold_in(key_list[7], 71), 0),
        "audio_k": draw_audio_k(jax.random.fold_in(key_list[7], 71), 0),
        "audio_v": noise(key_list[5], (AT, D), 1.0, 6.0, ((0, 32), (1, 8))),
        "align": draw_align(jax.random.fold_in(key_list[7], 71), 0),
    }


NEG = -1.0e30


def attend(queries, keys_self, values_self, keys_cross, values_cross, allowed):
    scale = HD ** -0.5
    qf = queries.astype(jnp.float32)
    first = jnp.dot(qf, keys_self.astype(jnp.float32).T, precision=lax.Precision.HIGHEST) * scale
    second = jnp.dot(qf, keys_cross.astype(jnp.float32).T, precision=lax.Precision.HIGHEST) * scale
    second = jnp.where(allowed, second, NEG)
    top = jnp.maximum(jnp.max(first, axis=-1), jnp.max(second, axis=-1))
    p_self = jnp.exp(first - top[:, None])
    p_cross = jnp.where(allowed, jnp.exp(second - top[:, None]), 0.0)
    total = jnp.sum(p_self, axis=-1) + jnp.sum(p_cross, axis=-1)
    w_self = lax.optimization_barrier(p_self.astype(jnp.bfloat16)).astype(jnp.float32)
    w_cross = lax.optimization_barrier(p_cross.astype(jnp.bfloat16)).astype(jnp.float32)
    summed = jnp.dot(w_self, values_self.astype(jnp.float32), precision=lax.Precision.HIGHEST)
    summed = summed + jnp.dot(w_cross, values_cross.astype(jnp.float32), precision=lax.Precision.HIGHEST)
    return (summed / total[:, None]).astype(jnp.bfloat16)


def split_heads(x):
    return x.reshape(x.shape[0], HEADS, HD).transpose(1, 0, 2)


def join_heads(x):
    return x.transpose(1, 0, 2).reshape(x.shape[1], HEADS * HD)


def reference(video_q, video_k, video_v, audio_q, audio_k, audio_v, align):
    audio_index = jnp.arange(AT, dtype=jnp.int32)
    video_rows = VT // N_SEQ

    def video_head(parts):
        qh, kh, vh, akh, avh = parts

        def block(item):
            rows, times = item
            allowed = jnp.abs(audio_index[None, :] - times[:, None]) <= WIN
            return attend(rows, kh, vh, akh, avh, allowed)

        out = lax.map(block, (qh.reshape(N_SEQ, video_rows, HD), align.reshape(N_SEQ, video_rows)))
        return out.reshape(VT, HD)

    def audio_head(parts):
        qh, kh, vh, akh, avh = parts

        def block(item):
            rows, where_at = item
            allowed = jnp.abs(align[None, :] - where_at[:, None]) <= WIN
            return attend(rows, akh, avh, kh, vh, allowed)

        out = lax.map(block, (qh.reshape(N_SEQ, A_DEV, HD), audio_index.reshape(N_SEQ, A_DEV)))
        return out.reshape(AT, HD)

    vk = split_heads(video_k)
    vv = split_heads(video_v)
    ak = split_heads(audio_k)
    av = split_heads(audio_v)
    video_out = lax.map(video_head, (split_heads(video_q), vk, vv, ak, av))
    audio_out = lax.map(audio_head, (split_heads(audio_q), vk, vv, ak, av))
    return join_heads(video_out), join_heads(audio_out)
```

```python
import functools

import jax
import jax.numpy as jnp
import numpy as np
from jax import lax
from jax.experimental import pallas as pl
from jax.experimental.pallas import tpu as pltpu
from jax.sharding import Mesh
from jax.sharding import PartitionSpec as P

HD = 128
HPG = 3
GW = HPG * HD
NZ, NX, NY, NC = 8, 4, 4, 2
TOK = 32
AUD = 16
VID = NZ * TOK
AUX = 16
QROWS = VID + AUD + AUX
KROWS = 2 * VID + 2 * AUD + AUX
NKB = NY * NC
WIN = 64.0
NEG = -1e30
C2 = HD**-0.5 * 1.4426950408889634
F32, BF16 = jnp.float32, jnp.bfloat16
VMEM = pl.BlockSpec(memory_space=pltpu.VMEM)
SMEM = pl.BlockSpec(memory_space=pltpu.SMEM)


def pack_body(pos_ref, align_ref, q_ref, k_ref, v_ref, kv_out, q_out):
    first = pos_ref[0]
    lane = lax.broadcasted_iota(jnp.int32, (1, GW), 1)
    row = jnp.zeros((1, GW), jnp.int32)
    for i in range(TOK):
        row = jnp.where(lane == first + i, align_ref[i], row)
    high = (row >> 4).astype(F32)
    low = (row & 15).astype(F32)
    which = lax.broadcasted_iota(jnp.int32, (AUX, GW), 0)
    aux = jnp.where(which == 0, high, jnp.where(which == 1, low, 0.0)).astype(BF16)
    for g in range(NZ):
        cols = slice(g * GW, (g + 1) * GW)
        kv_out[g, 0:TOK, :] = k_ref[:, cols]
        kv_out[g, TOK : 2 * TOK, :] = v_ref[:, cols]
        kv_out[g, 2 * TOK :, :] = aux
        q_out[g] = q_ref[:, cols]


def pack(pos, align, q, k, v):
    return pl.pallas_call(
        pack_body,
        out_shape=(
            jax.ShapeDtypeStruct((NZ, 2 * TOK + AUX, GW), BF16),
            jax.ShapeDtypeStruct((NZ, TOK, GW), BF16),
        ),
        in_specs=[SMEM, SMEM, VMEM, VMEM, VMEM],
        out_specs=(VMEM, VMEM),
        name="pack",
    )(pos, align, q, k, v)


def audio_times(start):
    lane = lax.broadcasted_iota(jnp.int32, (AUX, GW), 1) - VID
    which = lax.broadcasted_iota(jnp.int32, (AUX, GW), 0)
    stamp = lane + start
    here = (lane >= 0) & (lane < AUD)
    part = jnp.where(which == 0, stamp >> 4, jnp.where(which == 1, stamp & 15, 0))
    return jnp.where(here, part, 0).astype(F32)


def join_kv_body(pos_ref, kv_ref, aud_ref, out):
    total = audio_times(pos_ref[1])
    for g in range(NZ):
        out[g * TOK : (g + 1) * TOK, :] = kv_ref[g, 0:TOK, :]
        out[VID + g * TOK : VID + (g + 1) * TOK, :] = kv_ref[g, TOK : 2 * TOK, :]
        total = total + kv_ref[g, 2 * TOK :, :].astype(F32)
    out[2 * VID : 2 * VID + AUD, :] = aud_ref[:, GW : 2 * GW]
    out[2 * VID + AUD : 2 * VID + 2 * AUD, :] = aud_ref[:, 2 * GW :]
    out[2 * VID + 2 * AUD :, :] = total.astype(BF16)


def join_kv(pos, kv, aud):
    return pl.pallas_call(
        join_kv_body,
        out_shape=jax.ShapeDtypeStruct((KROWS, GW), BF16),
        in_specs=[SMEM, VMEM, VMEM],
        out_specs=VMEM,
        name="join_kv",
    )(pos, kv, aud)


def join_q_body(pos_ref, q_ref, kv_ref, aud_ref, out):
    total = audio_times(pos_ref[1])
    for g in range(NZ):
        out[g * TOK : (g + 1) * TOK, :] = q_ref[g]
        total = total + kv_ref[g, 2 * TOK :, :].astype(F32)
    out[VID : VID + AUD, :] = aud_ref[:, 0:GW]
    out[VID + AUD :, :] = total.astype(BF16)


def join_q(pos, q, kv, aud):
    return pl.pallas_call(
        join_q_body,
        out_shape=jax.ShapeDtypeStruct((QROWS, GW), BF16),
        in_specs=[SMEM, VMEM, VMEM, VMEM],
        out_specs=VMEM,
        name="join_q",
    )(pos, q, kv, aud)


def times_of(ref, first):
    aux = ref[first : first + AUX, :].astype(F32)
    return aux[0:1, :] * 16.0 + aux[1:2, :]


def as_column(row):
    return jnp.transpose(jnp.broadcast_to(row, (HD, HD)), (1, 0))


def place(rows):
    return sum(
        pltpu.roll(jnp.broadcast_to(row, (8, HD)), i * AUD, 1) if i else jnp.broadcast_to(row, (8, HD))
        for i, row in enumerate(rows)
    )[0:1, :]


def dot_nt(a, b):
    return lax.dot_general(a, b, (((1,), (1,)), ((), ())), preferred_element_type=F32)


def flash_body(*refs):
    q_refs = refs[0:NX]
    k_refs = refs[NX : NX + NKB]
    outs = refs[NX + NKB : NX + NKB + NX]
    ks, vs, s_ref = refs[NX + NKB + NX :]
    nkv = NKB * VID
    for j, k_ref in enumerate(k_refs):
        ks[j * VID : (j + 1) * VID, :] = k_ref[0:VID, :]
        vs[j * VID : (j + 1) * VID, :] = k_ref[VID : 2 * VID, :]
        at = nkv + j * AUD
        ks[at : at + AUD, :] = k_ref[2 * VID : 2 * VID + AUD, :]
        vs[at : at + AUD, :] = k_ref[2 * VID + AUD : 2 * VID + 2 * AUD, :]
    k_times = [times_of(k_ref, 2 * VID + 2 * AUD) for k_ref in k_refs]
    q_times = [times_of(q_ref, VID + AUD) for q_ref in q_refs]
    ka_times = place([t[:, VID:] for t in k_times])
    qa_times = place([t[:, VID:] for t in q_times])
    lane = lax.broadcasted_iota(jnp.int32, (1, HD), 1)

    def emit(out, r0, rows, h, cols, acc, top, total, src=0):
        out[r0 : r0 + rows, cols] = (acc / total).astype(BF16)[src : src + rows]
        lse = top * C2 + jnp.log2(total)
        hi = lse.astype(BF16).astype(F32)
        mid = (lse - hi).astype(BF16).astype(F32)
        lo = lse - hi - mid
        tile = jnp.where(lane == 3 * h, hi, jnp.where(lane == 3 * h + 1, mid, jnp.where(lane == 3 * h + 2, lo, 0.0)))
        old = out[r0 : r0 + rows, GW:].astype(F32)
        out[r0 : r0 + rows, GW:] = (old + tile[src : src + rows]).astype(BF16)

    for out in outs:
        out[:, GW:] = jnp.zeros((VID + AUD, HD), BF16)

    near = []
    for i in range(NX):
        column = jnp.concatenate(
            [as_column(q_times[i][:, a : a + HD]) for a in range(0, VID, HD)], axis=0
        )
        near.append(jnp.abs(column - ka_times) <= WIN)

    def video(i, h):
        cols = pl.ds(pl.multiple_of(h * HD, HD), HD)
        rows = q_refs[i][0:VID, cols]
        top = None
        for j in range(NKB):
            s = dot_nt(rows, ks[j * VID : (j + 1) * VID, cols])
            s_ref[:, j * VID : (j + 1) * VID] = s
            part = jnp.maximum(s[:, 0:HD], s[:, HD:])
            top = part if top is None else jnp.maximum(top, part)
        sa = jnp.where(near[i], dot_nt(rows, ks[nkv:, cols]), NEG)
        top = jnp.max(jnp.maximum(top, sa), axis=1, keepdims=True)
        pa = jnp.exp2((sa - top) * C2)
        total = pa
        acc = jnp.dot(pa.astype(BF16), vs[nkv:, cols], preferred_element_type=F32)
        for j in range(NKB):
            p = jnp.exp2((s_ref[:, j * VID : (j + 1) * VID] - top) * C2)
            total = total + p[:, 0:HD] + p[:, HD:]
            acc = acc + jnp.dot(
                p.astype(BF16), vs[j * VID : (j + 1) * VID, cols], preferred_element_type=F32
            )
        total = jnp.sum(total, axis=1, keepdims=True)
        emit(outs[i], 0, VID, h, cols, acc, top, total)

    def audio(h):
        n = NX * AUD
        cols = pl.ds(pl.multiple_of(h * HD, HD), HD)
        rows = jnp.concatenate([q_ref[VID : VID + AUD, cols] for q_ref in q_refs], axis=0)
        column = as_column(qa_times)[0:n, :]
        column = jnp.concatenate([column, column], axis=1)
        sa = dot_nt(rows, ks[nkv:, cols])
        top = sa
        for j in range(NKB):
            s = dot_nt(rows, ks[j * VID : (j + 1) * VID, cols])
            s = jnp.where(jnp.abs(column - k_times[j][:, 0:VID]) <= WIN, s, NEG)
            s_ref[0:n, j * VID : (j + 1) * VID] = s
            top = jnp.maximum(top, jnp.maximum(s[:, 0:HD], s[:, HD:]))
        top = jnp.max(top, axis=1, keepdims=True)
        pa = jnp.exp2((sa - top) * C2)
        total = pa
        acc = jnp.dot(pa.astype(BF16), vs[nkv:, cols], preferred_element_type=F32)
        for j in range(NKB):
            p = jnp.exp2((s_ref[0:n, j * VID : (j + 1) * VID] - top) * C2)
            total = total + p[:, 0:HD] + p[:, HD:]
            acc = acc + jnp.dot(
                p.astype(BF16), vs[j * VID : (j + 1) * VID, cols], preferred_element_type=F32
            )
        total = jnp.sum(total, axis=1, keepdims=True)
        for i in range(NX):
            emit(outs[i], VID, AUD, h, cols, acc, top, total, i * AUD)

    @pl.loop(0, HPG)
    def _(h):
        for i in range(NX):
            video(i, h)
        audio(h)


def flash(qs, kvs):
    nk = NKB * (VID + AUD)
    area = NX * (VID + AUD) * nk * HPG
    return pl.pallas_call(
        flash_body,
        out_shape=tuple(jax.ShapeDtypeStruct((VID + AUD, GW + HD), BF16) for _ in range(NX)),
        in_specs=[VMEM] * (NX + NKB),
        out_specs=tuple(VMEM for _ in range(NX)),
        scratch_shapes=[
            pltpu.VMEM((nk, GW), BF16),
            pltpu.VMEM((nk, GW), BF16),
            pltpu.VMEM((VID, NKB * VID), F32),
        ],
        compiler_params=pltpu.CompilerParams(vmem_limit_bytes=40 * 2**20),
        cost_estimate=pl.CostEstimate(flops=4 * area * HD, bytes_accessed=8 << 20, transcendentals=area),
        name="flash",
    )(*qs, *kvs)


def combine_body(a_ref, b_ref, c_ref, d_ref, video_out, audio_out):
    refs = (a_ref, b_ref, c_ref, d_ref)
    for h in range(HPG):
        lses = []
        for ref in refs:
            tile = ref[:, GW:].astype(F32)
            lses.append(tile[:, 3 * h : 3 * h + 1] + tile[:, 3 * h + 1 : 3 * h + 2] + tile[:, 3 * h + 2 : 3 * h + 3])
        top = functools.reduce(jnp.maximum, lses)
        weights = [jnp.exp2(x - top) for x in lses]
        scale = 1.0 / sum(weights)
        cols = slice(h * HD, (h + 1) * HD)
        out = sum(ref[:, cols].astype(F32) * (w * scale) for ref, w in zip(refs, weights, strict=True))
        out = out.astype(BF16)
        for g in range(NZ):
            video_out[g, :, cols] = out[g * TOK : (g + 1) * TOK]
        audio_out[:, cols] = out[VID:]


def combine(parts):
    return pl.pallas_call(
        combine_body,
        out_shape=(
            jax.ShapeDtypeStruct((NZ, TOK, GW), BF16),
            jax.ShapeDtypeStruct((AUD, GW), BF16),
        ),
        in_specs=[VMEM] * NX,
        out_specs=(VMEM, VMEM),
        name="combine",
    )(*parts)


def spread_body(in_ref, out_ref):
    for g in range(NZ):
        out_ref[:, g * GW : (g + 1) * GW] = in_ref[g]


def spread(x):
    return pl.pallas_call(
        spread_body,
        out_shape=jax.ShapeDtypeStruct((TOK, NZ * GW), BF16),
        in_specs=[VMEM],
        out_specs=VMEM,
        name="spread",
    )(x)


def shift(x, axis, n, k):
    return lax.ppermute(x, axis, [(i, (i + k) % n) for i in range(n)])


def swap_group(x):
    pairs = [(a * NZ + b, b * NZ + a) for a in range(NZ) for b in range(NZ)]
    return lax.ppermute(x, ("x", "yh", "z"), pairs)


def on_device(video_q, video_k, video_v, audio_q, audio_k, audio_v, align):
    ix, iyh, iyl = lax.axis_index("x"), lax.axis_index("yh"), lax.axis_index("yl")
    iz, ic = lax.axis_index("z"), lax.axis_index("c")
    block = iyl * 16 + (ix * 2 + iyh) * 2 + ic
    pos = jnp.stack([iz * TOK, block * AUD]).astype(jnp.int32)
    aud = swap_group(jnp.concatenate([audio_q, audio_k, audio_v], axis=1))
    kv_packed, q_packed = pack(pos, align, video_q, video_k, video_v)
    kv_got = lax.all_to_all(kv_packed, "z", split_axis=0, concat_axis=0, tiled=True)
    q_got = lax.all_to_all(q_packed, "z", split_axis=0, concat_axis=0, tiled=True)
    kv_own = join_kv(pos, kv_got, aud)
    q_own = join_q(pos, q_got, kv_got, aud)
    y = ("yh", "yl")
    kvs = [kv_own] + [shift(kv_own, y, NY, k) for k in (1, 3, 2)]
    qs = [q_own] + [shift(q_own, "x", NX, k) for k in (1, 3, 2)]
    kvs = kvs + [shift(b, "c", NC, 1) for b in kvs]
    parts = flash(qs, kvs)
    back = [parts[0]] + [shift(p, "x", NX, -k) for p, k in zip(parts[1:], (1, 3, 2), strict=True)]
    video, audio = combine(back)
    video = spread(lax.all_to_all(video, "z", split_axis=0, concat_axis=0, tiled=True))
    return video, swap_group(audio)


def solution(mesh):
    grid = Mesh(np.asarray(mesh.devices).reshape(4, 2, 2, 8, 2), ("x", "yh", "yl", "z", "c"))
    seq, head = ("yl", "z", "c"), ("x", "yh")
    rows = P(seq + head, None)
    audio = P(seq, head)
    return jax.shard_map(
        on_device,
        mesh=grid,
        in_specs=(rows, rows, rows, audio, audio, audio, P(seq + head)),
        out_specs=(rows, audio),
        check_vma=False,
    )
```

```python
import functools

import jax
import jax.numpy as jnp
import numpy as np
from jax import lax
from jax.experimental import pallas as pl
from jax.experimental.pallas import tpu as pltpu
from jax.sharding import Mesh
from jax.sharding import PartitionSpec as P

HD = 128
HPG = 3
GW = HPG * HD
NZ, NX, NY, NC = 8, 4, 4, 2
TOK = 32
AUD = 16
VID = NZ * TOK
AUX = 16
QROWS = VID + AUD + AUX
KROWS = 2 * VID + 2 * AUD + AUX
NKB = NY * NC
HALF = NKB // 2
WIN = 64.0
NEG = -1e30
C2 = HD**-0.5 * 1.4426950408889634
F32, BF16 = jnp.float32, jnp.bfloat16
VMEM = pl.BlockSpec(memory_space=pltpu.VMEM)
SMEM = pl.BlockSpec(memory_space=pltpu.SMEM)
SMALL = pltpu.CompilerParams(vmem_limit_bytes=6 * 2**20)


def pack_body(align_ref, q_ref, k_ref, v_ref, out):
    first = lax.axis_index("z") * TOK
    lane = lax.broadcasted_iota(jnp.int32, (1, GW), 1)
    row = jnp.zeros((1, GW), jnp.int32)
    for i in range(TOK):
        row = jnp.where(lane == first + i, align_ref[i], row)
    high = (row >> 4).astype(F32)
    low = (row & 15).astype(F32)
    which = lax.broadcasted_iota(jnp.int32, (AUX, GW), 0)
    aux = jnp.where(which == 0, high, jnp.where(which == 1, low, 0.0)).astype(BF16)
    for g in range(NZ):
        cols = slice(g * GW, (g + 1) * GW)
        out[g, 0:TOK, :] = q_ref[:, cols]
        out[g, TOK : 2 * TOK, :] = k_ref[:, cols]
        out[g, 2 * TOK : 3 * TOK, :] = v_ref[:, cols]
        out[g, 3 * TOK :, :] = aux


def pack(align, q, k, v):
    return pl.pallas_call(
        pack_body,
        out_shape=jax.ShapeDtypeStruct((NZ, 3 * TOK + AUX, GW), BF16),
        in_specs=[SMEM, VMEM, VMEM, VMEM],
        out_specs=VMEM,
        name="pack",
    )(align, q, k, v)


def audio_times(start):
    lane = lax.broadcasted_iota(jnp.int32, (AUX, GW), 1) - VID
    which = lax.broadcasted_iota(jnp.int32, (AUX, GW), 0)
    stamp = lane + start
    here = (lane >= 0) & (lane < AUD)
    part = jnp.where(which == 0, stamp >> 4, jnp.where(which == 1, stamp & 15, 0))
    return jnp.where(here, part, 0).astype(F32)


def join_body(got_ref, aud_ref, q_out, kv_out):
    block = lax.axis_index("yl") * 16 + (lax.axis_index("x") * 2 + lax.axis_index("yh")) * 2 + lax.axis_index("c")
    total = audio_times(block * AUD)
    for g in range(NZ):
        at = g * TOK
        q_out[at : at + TOK, :] = got_ref[g, 0:TOK, :]
        kv_out[at : at + TOK, :] = got_ref[g, TOK : 2 * TOK, :]
        kv_out[VID + at : VID + at + TOK, :] = got_ref[g, 2 * TOK : 3 * TOK, :]
        total = total + got_ref[g, 3 * TOK :, :].astype(F32)
    q_out[VID : VID + AUD, :] = aud_ref[:, 0:GW]
    kv_out[2 * VID : 2 * VID + AUD, :] = aud_ref[:, GW : 2 * GW]
    kv_out[2 * VID + AUD : 2 * VID + 2 * AUD, :] = aud_ref[:, 2 * GW :]
    q_out[VID + AUD :, :] = total.astype(BF16)
    kv_out[2 * VID + 2 * AUD :, :] = total.astype(BF16)


def join(got, aud):
    return pl.pallas_call(
        join_body,
        out_shape=(
            jax.ShapeDtypeStruct((QROWS, GW), BF16),
            jax.ShapeDtypeStruct((KROWS, GW), BF16),
        ),
        in_specs=[VMEM, VMEM],
        out_specs=(VMEM, VMEM),
        compiler_params=SMALL,
        name="join",
    )(got, aud)


def place(rows):
    return sum(
        pltpu.roll(jnp.broadcast_to(row, (8, HD)), i * AUD, 1) if i else jnp.broadcast_to(row, (8, HD))
        for i, row in enumerate(rows)
    )[0:1, :]


def dot_nt(a, b):
    return lax.dot_general(a, b, (((1,), (1,)), ((), ())), preferred_element_type=F32)


def dot_tn(a, b):
    return lax.dot_general(a, b, (((0,), (0,)), ((), ())), preferred_element_type=F32)


def times_of(ref, first):
    aux = ref[first : first + AUX, :].astype(F32)
    return aux[0:1, :] * 16.0 + aux[1:2, :]


def column_times(q_ref):
    which = lax.broadcasted_iota(jnp.int32, (AUX, HD), 0)
    pick = jnp.where(which == 0, 16.0, jnp.where(which == 1, 1.0, 0.0)).astype(BF16)
    return dot_tn(q_ref[VID + AUD :, :], pick)


def side_by_side(x):
    return jnp.concatenate([x, x], axis=1)


def scores(q, k_refs, cols, near_audio, s_ref, h):
    top = None
    for j, k_ref in enumerate(k_refs):
        s = dot_nt(q, k_ref[0:VID, cols])
        s = jnp.concatenate([s[0:VID], jnp.where(near_audio[j], s[VID:], NEG)], axis=0)
        s_ref[h, :, j * VID : (j + 1) * VID] = s
        part = jnp.maximum(s[:, 0:HD], s[:, HD:])
        top = part if top is None else jnp.maximum(top, part)
    return top


def weigh(s, top, v, ones):
    p = jnp.exp2((s - top) * C2).astype(BF16)
    v = jnp.concatenate([v, ones[0 : v.shape[0]]], axis=1)
    return jnp.dot(p, v, preferred_element_type=F32)


def early_body(*refs):
    q_refs, k_refs = refs[0:NX], refs[NX : NX + HALF]
    outs, s_ref = refs[NX + HALF : NX + HALF + 2 * NX], refs[-1]
    k_times = [times_of(k_ref, 2 * VID + 2 * AUD) for k_ref in k_refs]
    ones = jnp.ones((VID, HD), BF16)

    def start(i, h):
        q_ref = q_refs[i]
        cols = slice(h * HD, (h + 1) * HD)
        column = side_by_side(column_times(q_ref)[VID : VID + AUD])
        near_audio = [jnp.abs(column - t[:, 0:VID]) <= WIN for t in k_times]
        top = scores(q_ref[0 : VID + AUD, cols], k_refs, cols, near_audio, s_ref, (i * HPG + h) % 3)
        return jnp.max(top, axis=1, keepdims=True)

    def end(i, h, top):
        cols = slice(h * HD, (h + 1) * HD)
        acc = 0.0
        for j, k_ref in enumerate(k_refs):
            s = s_ref[(i * HPG + h) % 3, :, j * VID : (j + 1) * VID]
            acc = acc + weigh(s, top, k_ref[VID : 2 * VID, cols], ones)
        total = acc[:, HD:]
        outs[2 * i][:, cols] = acc[:, 0:HD] / total
        outs[2 * i + 1][:, cols] = top * C2 + jnp.log2(total)

    work = [(i, h) for i in range(NX) for h in range(HPG)]
    tops = {}
    for n, item in enumerate(work):
        tops[item] = start(*item)
        if n >= 2:
            end(*work[n - 2], tops[work[n - 2]])
    for item in work[-2:]:
        end(*item, tops[item])


def early(qs, kvs):
    rows, nk = VID + AUD, HALF * VID
    area = NX * rows * nk * HPG
    return pl.pallas_call(
        early_body,
        out_shape=tuple(jax.ShapeDtypeStruct((rows, GW), F32) for _ in range(2 * NX)),
        in_specs=[VMEM] * (NX + HALF),
        out_specs=tuple(VMEM for _ in range(2 * NX)),
        scratch_shapes=[pltpu.VMEM((3, rows, nk), F32)],
        compiler_params=pltpu.CompilerParams(vmem_limit_bytes=16 * 2**20),
        cost_estimate=pl.CostEstimate(flops=6 * area * HD, bytes_accessed=4 << 20, transcendentals=area),
        name="early",
    )(*qs, *kvs)


def late_body(q_ref, o_ref, l_ref, *refs):
    k_refs, out, s_ref = refs[0:NKB], refs[NKB], refs[NKB + 1]
    rows = VID + AUD
    half = k_refs[HALF:]
    ka_times = place([times_of(k_ref, 2 * VID + 2 * AUD)[:, VID:] for k_ref in k_refs])
    k_times = [times_of(k_ref, 2 * VID + 2 * AUD) for k_ref in half]
    column = column_times(q_ref)
    near_video = jnp.abs(column[0:VID] - ka_times) <= WIN
    column = side_by_side(column[VID:rows])
    near_audio = [jnp.abs(column - t[:, 0:VID]) <= WIN for t in k_times]
    ones = jnp.ones((VID, HD), BF16)
    eye = lax.broadcasted_iota(jnp.int32, (HD, HD), 0) == lax.broadcasted_iota(jnp.int32, (HD, HD), 1)
    which = lax.broadcasted_iota(jnp.int32, (AUX, GW), 0)
    first = HALF * VID

    def start(h):
        cols = slice(h * HD, (h + 1) * HD)
        q = q_ref[0:rows, cols]
        top = scores(q, half, cols, near_audio, s_ref, h)
        s = dot_nt(q, jnp.concatenate([k[2 * VID : 2 * VID + AUD, cols] for k in k_refs], axis=0))
        s = jnp.concatenate([jnp.where(near_video, s[0:VID], NEG), s[VID:]], axis=0)
        s_ref[h, :, first:] = s
        return jnp.max(jnp.maximum(top, s), axis=1, keepdims=True)

    def end(h, top):
        cols = slice(h * HD, (h + 1) * HD)
        at = 2 * VID + AUD
        acc = weigh(s_ref[h, :, first:], top, jnp.concatenate([k[at : at + AUD, cols] for k in k_refs], axis=0), ones)
        for j, k_ref in enumerate(half):
            acc = acc + weigh(s_ref[h, :, j * VID : (j + 1) * VID], top, k_ref[VID : 2 * VID, cols], ones)
        base = top * C2
        before = l_ref[:, cols]
        most = jnp.maximum(base, before)
        w_here, w_before = jnp.exp2(base - most), jnp.exp2(before - most)
        total = acc[:, HD:] * w_here + w_before
        out[0:rows, cols] = ((acc[:, 0:HD] * w_here + o_ref[:, cols] * w_before) / total).astype(BF16)
        lse = most + jnp.log2(total)
        row = jnp.concatenate(
            [
                jnp.sum(jnp.where(eye[0:n], lse[a : a + n], 0.0), axis=0, keepdims=True)
                for a, n in ((0, HD), (HD, HD), (VID, AUD))
            ],
            axis=1,
        )
        hi = row.astype(BF16).astype(F32)
        mid = (row - hi).astype(BF16).astype(F32)
        low = row - hi - mid
        return jnp.where(which == 3 * h, hi, jnp.where(which == 3 * h + 1, mid, jnp.where(which == 3 * h + 2, low, 0.0)))

    tops = [start(h) for h in range(HPG)]
    out[rows:, :] = sum(end(h, tops[h]) for h in range(HPG)).astype(BF16)


def late(q, state, kvs):
    rows, nk = VID + AUD, HALF * VID + NKB * AUD
    area = rows * nk * HPG
    return pl.pallas_call(
        late_body,
        out_shape=jax.ShapeDtypeStruct((QROWS, GW), BF16),
        in_specs=[VMEM] * (3 + NKB),
        out_specs=VMEM,
        scratch_shapes=[pltpu.VMEM((HPG, rows, nk), F32)],
        compiler_params=pltpu.CompilerParams(vmem_limit_bytes=16 * 2**20),
        cost_estimate=pl.CostEstimate(flops=6 * area * HD, bytes_accessed=5 << 20, transcendentals=area),
        name="late",
    )(q, *state, *kvs)


def combine_body(a_ref, b_ref, c_ref, d_ref, video_out, audio_out):
    refs = (a_ref, b_ref, c_ref, d_ref)
    rows = VID + AUD
    which = lax.broadcasted_iota(jnp.int32, (AUX, HD), 0)
    for h in range(HPG):
        pick = jnp.where((which >= 3 * h) & (which < 3 * h + 3), 1.0, 0.0).astype(BF16)
        lses = [dot_tn(ref[rows:, :], pick)[0:rows] for ref in refs]
        top = functools.reduce(jnp.maximum, lses)
        weights = [jnp.exp2(x - top) for x in lses]
        scale = 1.0 / sum(weights)
        cols = slice(h * HD, (h + 1) * HD)
        out = sum(ref[0:rows, cols].astype(F32) * (w * scale) for ref, w in zip(refs, weights, strict=True))
        out = out.astype(BF16)
        for g in range(NZ):
            video_out[g, :, cols] = out[g * TOK : (g + 1) * TOK]
        audio_out[:, cols] = out[VID:]


def combine(parts):
    return pl.pallas_call(
        combine_body,
        out_shape=(
            jax.ShapeDtypeStruct((NZ, TOK, GW), BF16),
            jax.ShapeDtypeStruct((AUD, GW), BF16),
        ),
        in_specs=[VMEM] * NX,
        out_specs=(VMEM, VMEM),
        compiler_params=SMALL,
        name="combine",
    )(*parts)


def shift(x, axis, n, k):
    return lax.ppermute(x, axis, [(i, (i + k) % n) for i in range(n)])


def swap_group(x):
    pairs = [(a * NZ + b, b * NZ + a) for a in range(NZ) for b in range(NZ)]
    return lax.ppermute(x, ("x", "yh", "z"), pairs)


def on_device(video_q, video_k, video_v, audio_q, audio_k, audio_v, align):
    aud = swap_group(jnp.concatenate([audio_q, audio_k, audio_v], axis=1))
    got = lax.all_to_all(
        pack(align, video_q, video_k, video_v), "z", split_axis=0, concat_axis=0, tiled=True
    )
    q_own, kv_own = join(got, aud)
    y = ("yh", "yl")
    core = functools.partial(shift, axis="c", n=NC, k=1)
    far, near = shift(kv_own, y, NY, 2), core(kv_own)
    qs = [shift(q_own, "x", NX, k) for k in (2, 1, 3)]
    right, left = [shift(kv_own, y, NY, k) for k in (1, 3)]
    qs = qs + [q_own]
    first = [kv_own, far, near, core(far)]
    state = early(qs, first)
    kvs = first + [right, left, core(right), core(left)]
    parts = [late(q, state[2 * i : 2 * i + 2], kvs) for i, q in enumerate(qs)]
    back = [shift(p, "x", NX, -k) for p, k in zip(parts, (2, 1, 3))]
    video, audio = combine(parts[3:] + back)
    video = lax.all_to_all(video, "z", split_axis=0, concat_axis=0, tiled=True)
    return video.transpose(1, 0, 2).reshape(TOK, NZ * GW), swap_group(audio)


def solution(mesh):
    grid = Mesh(np.asarray(mesh.devices).reshape(4, 2, 2, 8, 2), ("x", "yh", "yl", "z", "c"))
    seq, head = ("yl", "z", "c"), ("x", "yh")
    rows = P(seq + head, None)
    audio = P(seq, head)
    return jax.shard_map(
        on_device,
        mesh=grid,
        in_specs=(rows, rows, rows, audio, audio, audio, P(seq + head)),
        out_specs=(rows, audio),
        check_vma=False,
    )
```

```python
import functools

import jax
import jax.numpy as jnp
import numpy as np
from jax import lax
from jax.experimental import pallas as pl
from jax.experimental.pallas import tpu as pltpu
from jax.sharding import Mesh
from jax.sharding import PartitionSpec as P

HD = 128
HPG = 3
GW = HPG * HD
NZ, NX, NY, NC = 8, 4, 4, 2
TOK = 32
AUD = 16
VID = NZ * TOK
AUX = 16
QROWS = VID + AUD + AUX
KROWS = 2 * VID + 2 * AUD + AUX
NKB = NY * NC
EARLY = 6
WIN = 64.0
NEG = -1e30
C2 = HD**-0.5 * 1.4426950408889634
F32, BF16 = jnp.float32, jnp.bfloat16
VMEM = pl.BlockSpec(memory_space=pltpu.VMEM)
SMEM = pl.BlockSpec(memory_space=pltpu.SMEM)
SMALL = pltpu.CompilerParams(vmem_limit_bytes=6 * 2**20)


def pack_body(align_ref, q_ref, k_ref, v_ref, out):
    first = lax.axis_index("z") * TOK
    lane = lax.broadcasted_iota(jnp.int32, (1, GW), 1)
    row = jnp.zeros((1, GW), jnp.int32)
    for i in range(TOK):
        row = jnp.where(lane == first + i, align_ref[i], row)
    high = (row >> 4).astype(F32)
    low = (row & 15).astype(F32)
    which = lax.broadcasted_iota(jnp.int32, (AUX, GW), 0)
    aux = jnp.where(which == 0, high, jnp.where(which == 1, low, 0.0)).astype(BF16)
    for g in range(NZ):
        cols = slice(g * GW, (g + 1) * GW)
        out[g, 0:TOK, :] = q_ref[:, cols]
        out[g, TOK : 2 * TOK, :] = k_ref[:, cols]
        out[g, 2 * TOK : 3 * TOK, :] = v_ref[:, cols]
        out[g, 3 * TOK :, :] = aux


def pack(align, q, k, v):
    return pl.pallas_call(
        pack_body,
        out_shape=jax.ShapeDtypeStruct((NZ, 3 * TOK + AUX, GW), BF16),
        in_specs=[SMEM, VMEM, VMEM, VMEM],
        out_specs=VMEM,
        name="pack",
    )(align, q, k, v)


def audio_times(start):
    lane = lax.broadcasted_iota(jnp.int32, (AUX, GW), 1) - VID
    which = lax.broadcasted_iota(jnp.int32, (AUX, GW), 0)
    stamp = lane + start
    here = (lane >= 0) & (lane < AUD)
    part = jnp.where(which == 0, stamp >> 4, jnp.where(which == 1, stamp & 15, 0))
    return jnp.where(here, part, 0).astype(F32)


def join_body(got_ref, aud_ref, q_out, kv_out):
    block = lax.axis_index("yl") * 16 + audio_z() * 2 + lax.axis_index("c")
    total = audio_times(block * AUD)
    for g in range(NZ):
        at = g * TOK
        q_out[at : at + TOK, :] = got_ref[g, 0:TOK, :]
        kv_out[at : at + TOK, :] = got_ref[g, TOK : 2 * TOK, :]
        kv_out[VID + at : VID + at + TOK, :] = got_ref[g, 2 * TOK : 3 * TOK, :]
        total = total + got_ref[g, 3 * TOK :, :].astype(F32)
    q_out[VID : VID + AUD, :] = aud_ref[:, 0:GW]
    kv_out[2 * VID : 2 * VID + AUD, :] = aud_ref[:, GW : 2 * GW]
    kv_out[2 * VID + AUD : 2 * VID + 2 * AUD, :] = aud_ref[:, 2 * GW :]
    q_out[VID + AUD :, :] = total.astype(BF16)
    kv_out[2 * VID + 2 * AUD :, :] = total.astype(BF16)


def join(got, aud):
    return pl.pallas_call(
        join_body,
        out_shape=(
            pltpu.VMEM((QROWS, GW), BF16),
            pltpu.VMEM((KROWS, GW), BF16),
        ),
        in_specs=[VMEM, VMEM],
        out_specs=(VMEM, VMEM),
        compiler_params=SMALL,
        name="join",
    )(got, aud)


def place(rows):
    return sum(
        pltpu.roll(jnp.broadcast_to(row, (8, HD)), i * AUD, 1) if i else jnp.broadcast_to(row, (8, HD))
        for i, row in enumerate(rows)
    )[0:1, :]


def dot_nt(a, b):
    return lax.dot_general(a, b, (((1,), (1,)), ((), ())), preferred_element_type=F32)


def dot_tn(a, b):
    return lax.dot_general(a, b, (((0,), (0,)), ((), ())), preferred_element_type=F32)


def times_of(ref, first):
    aux = ref[first : first + AUX, :].astype(F32)
    return aux[0:1, :] * 16.0 + aux[1:2, :]


def column_times(q_ref):
    which = lax.broadcasted_iota(jnp.int32, (AUX, HD), 0)
    pick = jnp.where(which == 0, 16.0, jnp.where(which == 1, 1.0, 0.0)).astype(BF16)
    return dot_tn(q_ref[VID + AUD : QROWS, :], pick)


def side_by_side(x):
    return jnp.concatenate([x, x], axis=1)


def scores(q, k_refs, cols, near_audio, s_ref, h):
    top = None
    for j, k_ref in enumerate(k_refs):
        s = dot_nt(q, k_ref[0:VID, cols])
        s = jnp.concatenate([s[0:VID], jnp.where(near_audio[j], s[VID:], NEG)], axis=0)
        s_ref[h, :, j * VID : (j + 1) * VID] = s
        part = jnp.maximum(s[:, 0:HD], s[:, HD:])
        top = part if top is None else jnp.maximum(top, part)
    return top


def weigh(s, top, v, ones):
    p = jnp.exp2((s - top) * C2).astype(BF16)
    v = jnp.concatenate([v, ones[0 : v.shape[0]]], axis=1)
    return jnp.dot(p, v, preferred_element_type=F32)


def early_body(*refs):
    n = (len(refs) - EARLY - 1) // 3
    q_refs, k_refs = refs[0:n], refs[n : n + EARLY]
    outs, s_ref = refs[n + EARLY : -1], refs[-1]
    k_times = [times_of(k_ref, 2 * VID + 2 * AUD) for k_ref in k_refs]
    ones = jnp.ones((VID, HD), BF16)

    def start(i, h):
        q_ref = q_refs[i]
        cols = slice(h * HD, (h + 1) * HD)
        column = side_by_side(column_times(q_ref)[VID : VID + AUD])
        near_audio = [jnp.abs(column - t[:, 0:VID]) <= WIN for t in k_times]
        top = scores(q_ref[0 : VID + AUD, cols], k_refs, cols, near_audio, s_ref, (i * HPG + h) % 3)
        return jnp.max(top, axis=1, keepdims=True)

    def end(i, h, top):
        cols = slice(h * HD, (h + 1) * HD)
        acc = 0.0
        for j, k_ref in enumerate(k_refs):
            s = s_ref[(i * HPG + h) % 3, :, j * VID : (j + 1) * VID]
            acc = acc + weigh(s, top, k_ref[VID : 2 * VID, cols], ones)
        total = acc[:, HD:]
        outs[2 * i][:, cols] = acc[:, 0:HD] / total
        outs[2 * i + 1][:, cols] = top * C2 + jnp.log2(total)

    work = [(i, h) for i in range(n) for h in range(HPG)]
    tops = {}
    for m, item in enumerate(work):
        tops[item] = start(*item)
        if m >= 2:
            end(*work[m - 2], tops[work[m - 2]])
    for item in work[-2:]:
        end(*item, tops[item])


def early(qs, kvs):
    n, rows, nk = len(qs), VID + AUD, EARLY * VID
    area = n * rows * nk * HPG
    return pl.pallas_call(
        early_body,
        out_shape=tuple(jax.ShapeDtypeStruct((rows, GW), F32) for _ in range(2 * n)),
        in_specs=[VMEM] * (n + EARLY),
        out_specs=tuple(VMEM for _ in range(2 * n)),
        scratch_shapes=[pltpu.VMEM((3, rows, nk), F32)],
        compiler_params=pltpu.CompilerParams(vmem_limit_bytes=16 * 2**20),
        cost_estimate=pl.CostEstimate(flops=6 * area * HD, bytes_accessed=4 << 20, transcendentals=area),
        name="early",
    )(*qs, *kvs)


def late_body(q_ref, o_ref, l_ref, *refs):
    out, s_ref, far_ref, twin_ref = refs[EARLY + 4 :]
    rows = VID + AUD
    for n, ref in enumerate((far_ref, twin_ref)):
        ref[0:VID, :] = refs[EARLY + 2 * n][...]
        ref[VID:, :] = refs[EARLY + 2 * n + 1][...]
    rest = (far_ref, twin_ref)
    k_refs = refs[0:EARLY] + rest
    ka_times = place([times_of(k_ref, 2 * VID + 2 * AUD)[:, VID:] for k_ref in k_refs])
    k_times = [times_of(k_ref, 2 * VID + 2 * AUD) for k_ref in rest]
    column = column_times(q_ref)
    near_video = jnp.abs(column[0:VID] - ka_times) <= WIN
    column = side_by_side(column[VID:rows])
    near_audio = [jnp.abs(column - t[:, 0:VID]) <= WIN for t in k_times]
    ones = jnp.ones((VID, HD), BF16)
    eye = lax.broadcasted_iota(jnp.int32, (HD, HD), 0) == lax.broadcasted_iota(jnp.int32, (HD, HD), 1)
    which = lax.broadcasted_iota(jnp.int32, (AUX, GW), 0)
    first = len(rest) * VID

    def start(h):
        cols = slice(h * HD, (h + 1) * HD)
        q = q_ref[0:rows, cols]
        top = scores(q, rest, cols, near_audio, s_ref, h)
        s = dot_nt(q, jnp.concatenate([k[2 * VID : 2 * VID + AUD, cols] for k in k_refs], axis=0))
        s = jnp.concatenate([jnp.where(near_video, s[0:VID], NEG), s[VID:]], axis=0)
        s_ref[h, :, first:] = s
        return jnp.max(jnp.maximum(top, s), axis=1, keepdims=True)

    def end(h, top):
        cols = slice(h * HD, (h + 1) * HD)
        at = 2 * VID + AUD
        acc = weigh(s_ref[h, :, first:], top, jnp.concatenate([k[at : at + AUD, cols] for k in k_refs], axis=0), ones)
        for j, k_ref in enumerate(rest):
            acc = acc + weigh(s_ref[h, :, j * VID : (j + 1) * VID], top, k_ref[VID : 2 * VID, cols], ones)
        base = top * C2
        before = l_ref[:, cols]
        most = jnp.maximum(base, before)
        w_here, w_before = jnp.exp2(base - most), jnp.exp2(before - most)
        total = acc[:, HD:] * w_here + w_before
        out[0:rows, cols] = ((acc[:, 0:HD] * w_here + o_ref[:, cols] * w_before) / total).astype(BF16)
        lse = most + jnp.log2(total)
        row = jnp.concatenate(
            [
                jnp.sum(jnp.where(eye[0:n], lse[a : a + n], 0.0), axis=0, keepdims=True)
                for a, n in ((0, HD), (HD, HD), (VID, AUD))
            ],
            axis=1,
        )
        hi = row.astype(BF16).astype(F32)
        mid = (row - hi).astype(BF16).astype(F32)
        low = row - hi - mid
        return jnp.where(which == 3 * h, hi, jnp.where(which == 3 * h + 1, mid, jnp.where(which == 3 * h + 2, low, 0.0)))

    tops = [start(h) for h in range(HPG)]
    out[rows:, :] = sum(end(h, tops[h]) for h in range(HPG)).astype(BF16)


def late(q, state, kvs):
    rows, nk = VID + AUD, (NKB - EARLY) * VID + NKB * AUD
    area = rows * nk * HPG
    return pl.pallas_call(
        late_body,
        out_shape=jax.ShapeDtypeStruct((QROWS, GW), BF16),
        in_specs=[VMEM] * (3 + EARLY + 4),
        out_specs=VMEM,
        scratch_shapes=[
            pltpu.VMEM((HPG, rows, nk), F32),
            pltpu.VMEM((KROWS, GW), BF16),
            pltpu.VMEM((KROWS, GW), BF16),
        ],
        compiler_params=pltpu.CompilerParams(vmem_limit_bytes=16 * 2**20),
        cost_estimate=pl.CostEstimate(flops=6 * area * HD, bytes_accessed=5 << 20, transcendentals=area),
        name="late",
    )(q, *state, *kvs)


def combine_body(a_ref, b_ref, c_ref, d_ref, video_out, audio_out):
    refs = (a_ref, b_ref, c_ref, d_ref)
    rows = VID + AUD
    which = lax.broadcasted_iota(jnp.int32, (AUX, HD), 0)
    for h in range(HPG):
        pick = jnp.where((which >= 3 * h) & (which < 3 * h + 3), 1.0, 0.0).astype(BF16)
        lses = [dot_tn(ref[rows:, :], pick)[0:rows] for ref in refs]
        top = functools.reduce(jnp.maximum, lses)
        weights = [jnp.exp2(x - top) for x in lses]
        scale = 1.0 / sum(weights)
        cols = slice(h * HD, (h + 1) * HD)
        out = sum(ref[0:rows, cols].astype(F32) * (w * scale) for ref, w in zip(refs, weights, strict=True))
        out = out.astype(BF16)
        for g in range(NZ):
            video_out[g, :, cols] = out[g * TOK : (g + 1) * TOK]
        audio_out[:, cols] = out[VID:]


def combine(parts):
    return pl.pallas_call(
        combine_body,
        out_shape=(
            jax.ShapeDtypeStruct((NZ, TOK, GW), BF16),
            jax.ShapeDtypeStruct((AUD, GW), BF16),
        ),
        in_specs=[VMEM] * NX,
        out_specs=(VMEM, VMEM),
        compiler_params=SMALL,
        name="combine",
    )(*parts)


def shift(x, axis, n, k):
    return lax.ppermute(x, axis, [(i, (i + k) % n) for i in range(n)])


PLACES = ((2, 1), (1, 1), (2, 0), (1, 0), (0, 0), (3, 0), (0, 1), (3, 1))


def audio_pairs():
    pairs = []
    for group in range(NZ):
        for ahead, (dx, dy) in enumerate(PLACES):
            there = ((group // 2 + dx) % NX) * 2 + (group % 2 + dy) % 2
            pairs.append((group * NZ + (group + ahead) % NZ, there * NZ + group))
    return pairs


def audio_z():
    group = lax.axis_index("z")
    dx = lax.rem(lax.axis_index("x") + NX - group // 2, NX)
    dy = lax.rem(lax.axis_index("yh") + 2 - lax.rem(group, 2), 2)
    ahead = 0
    for n, (px, py) in enumerate(PLACES):
        ahead = jnp.where((dx == px) & (dy == py), n, ahead)
    return lax.rem(group + ahead, NZ)


def to_group(x):
    return lax.ppermute(x, ("x", "yh", "z"), audio_pairs())


def from_group(x):
    return lax.ppermute(x, ("x", "yh", "z"), [(b, a) for a, b in audio_pairs()])


def on_device(video_q, video_k, video_v, audio_q, audio_k, audio_v, align):
    aud = to_group(jnp.concatenate([audio_q, audio_k, audio_v], axis=1))
    got = lax.all_to_all(
        pack(align, video_q, video_k, video_v), "z", split_axis=0, concat_axis=0, tiled=True
    )
    q_own, kv_own = join(got, aud)
    y = ("yh", "yl")
    core = functools.partial(shift, axis="c", n=NC, k=1)
    right, left = [shift(kv_own, y, NY, k) for k in (1, 3)]
    q_right, q_left = [shift(q_own, "x", NX, k) for k in (1, 3)]
    got = lax.optimization_barrier([left, right, q_left, q_right, q_own, kv_own])
    left, right, q_left, q_right, q_own, kv_own = got
    far = [shift(right[0:VID], y, NY, 1), shift(left[VID:], y, NY, 3)]
    q_far = shift(q_right, "x", NX, 1)
    kvs = [kv_own, right, left] + [core(b) for b in (kv_own, right, left)]
    state = early([q_right, q_left, q_own], kvs)
    q_far, state = lax.optimization_barrier((q_far, state))
    state_far = early([q_far], kvs)
    far, state_far = lax.optimization_barrier((far, state_far))
    kvs = kvs + far + [core(b) for b in far]
    states = [state_far, state[0:2], state[2:4], state[4:6]]
    parts = [late(q, st, kvs) for q, st in zip([q_far, q_right, q_left, q_own], states)]
    back = [shift(p, "x", NX, -k) for p, k in zip(parts, (2, 1, 3))]
    video, audio = combine(parts[3:] + back)
    video = lax.all_to_all(video, "z", split_axis=0, concat_axis=0, tiled=True)
    return video.transpose(1, 0, 2).reshape(TOK, NZ * GW), from_group(audio)


def solution(mesh):
    grid = Mesh(np.asarray(mesh.devices).reshape(4, 2, 2, 8, 2), ("x", "yh", "yl", "z", "c"))
    seq, head = ("yl", "z", "c"), ("x", "yh")
    rows = P(seq + head, None)
    audio = P(seq, head)
    return jax.shard_map(
        on_device,
        mesh=grid,
        in_specs=(rows, rows, rows, audio, audio, audio, P(seq + head)),
        out_specs=(rows, audio),
        check_vma=False,
    )
```

```python
import functools

import jax
import jax.numpy as jnp
import numpy as np
from jax import lax
from jax.experimental import pallas as pl
from jax.experimental.pallas import tpu as pltpu
from jax.sharding import Mesh
from jax.sharding import PartitionSpec as P

HD = 128
HPG = 3
GW = HPG * HD
NZ, NX, NY, NC = 8, 4, 4, 2
TOK = 32
AUD = 16
VID = NZ * TOK
STAMPS = 8
AUX = 16
QROWS = VID + AUD + AUX
KROWS = 2 * VID + 2 * AUD + AUX
NKB = NY * NC
EARLY = 6
WIN = 64.0
NEG = -1e30
C2 = HD**-0.5 * 1.4426950408889634
F32, BF16 = jnp.float32, jnp.bfloat16
VMEM = pl.BlockSpec(memory_space=pltpu.VMEM)
SMEM = pl.BlockSpec(memory_space=pltpu.SMEM)
ANY = pl.BlockSpec(memory_space=pl.ANY)
SMALL = pltpu.CompilerParams(vmem_limit_bytes=6 * 2**20)


def pack_body(align_ref, q_ref, k_ref, v_ref, out):
    first = lax.axis_index("z") * TOK
    lane = lax.broadcasted_iota(jnp.int32, (1, GW), 1)
    row = jnp.zeros((1, GW), jnp.int32)
    for i in range(TOK):
        row = jnp.where(lane == first + i, align_ref[i], row)
    high = (row >> 4).astype(F32)
    low = (row & 15).astype(F32)
    which = lax.broadcasted_iota(jnp.int32, (STAMPS, GW), 0)
    stamps = jnp.where(which == 0, high, jnp.where(which == 1, low, 0.0)).astype(BF16)
    for g in range(NZ):
        cols = slice(g * GW, (g + 1) * GW)
        out[g, 0:TOK, :] = q_ref[:, cols]
        out[g, TOK : 2 * TOK, :] = k_ref[:, cols]
        out[g, 2 * TOK : 3 * TOK, :] = v_ref[:, cols]
        out[g, 3 * TOK :, :] = stamps


def pack(align, q, k, v):
    return pl.pallas_call(
        pack_body,
        out_shape=jax.ShapeDtypeStruct((NZ, 3 * TOK + STAMPS, GW), BF16),
        in_specs=[SMEM, VMEM, VMEM, VMEM],
        out_specs=VMEM,
        name="pack",
    )(align, q, k, v)


def audio_times(start):
    lane = lax.broadcasted_iota(jnp.int32, (STAMPS, GW), 1) - VID
    which = lax.broadcasted_iota(jnp.int32, (STAMPS, GW), 0)
    stamp = lane + start
    here = (lane >= 0) & (lane < AUD)
    part = jnp.where(which == 0, stamp >> 4, jnp.where(which == 1, stamp & 15, 0))
    return jnp.where(here, part, 0).astype(F32)


def join_body(got_ref, aud_ref, q_out, kv_out):
    block = lax.axis_index("yl") * 16 + audio_z() * 2 + lax.axis_index("c")
    total = audio_times(block * AUD)
    for g in range(NZ):
        at = g * TOK
        q_out[at : at + TOK, :] = got_ref[g, 0:TOK, :]
        kv_out[at : at + TOK, :] = got_ref[g, TOK : 2 * TOK, :]
        kv_out[VID + at : VID + at + TOK, :] = got_ref[g, 2 * TOK : 3 * TOK, :]
        total = total + got_ref[g, 3 * TOK :, :].astype(F32)
    total = jnp.concatenate([total, jnp.zeros((AUX - STAMPS, GW), F32)], axis=0)
    q_out[VID : VID + AUD, :] = aud_ref[:, 0:GW]
    kv_out[2 * VID : 2 * VID + AUD, :] = aud_ref[:, GW : 2 * GW]
    kv_out[2 * VID + AUD : 2 * VID + 2 * AUD, :] = aud_ref[:, 2 * GW :]
    q_out[VID + AUD :, :] = total.astype(BF16)
    kv_out[2 * VID + 2 * AUD :, :] = total.astype(BF16)


def join(got, aud):
    return pl.pallas_call(
        join_body,
        out_shape=(
            pltpu.VMEM((QROWS, GW), BF16),
            pltpu.VMEM((KROWS, GW), BF16),
        ),
        in_specs=[VMEM, VMEM],
        out_specs=(VMEM, VMEM),
        compiler_params=SMALL,
        name="join",
    )(got, aud)


def place(rows):
    return sum(
        pltpu.roll(jnp.broadcast_to(row, (8, HD)), i * AUD, 1) if i else jnp.broadcast_to(row, (8, HD))
        for i, row in enumerate(rows)
    )[0:1, :]


def dot_nt(a, b):
    return lax.dot_general(a, b, (((1,), (1,)), ((), ())), preferred_element_type=F32)


def dot_tn(a, b):
    return lax.dot_general(a, b, (((0,), (0,)), ((), ())), preferred_element_type=F32)


def times_of(ref, first):
    aux = ref[first : first + AUX, :].astype(F32)
    return aux[0:1, :] * 16.0 + aux[1:2, :]


def column_times(q_ref):
    which = lax.broadcasted_iota(jnp.int32, (AUX, HD), 0)
    pick = jnp.where(which == 0, 16.0, jnp.where(which == 1, 1.0, 0.0)).astype(BF16)
    return dot_tn(q_ref[VID + AUD : QROWS, :], pick)


def side_by_side(x):
    return jnp.concatenate([x, x], axis=1)


def scores(q, k_refs, cols, near_audio, s_ref, h):
    top = None
    for j, k_ref in enumerate(k_refs):
        s = dot_nt(q, k_ref[0:VID, cols])
        s = jnp.concatenate([s[0:VID], jnp.where(near_audio[j], s[VID:], NEG)], axis=0)
        s_ref[h, :, j * VID : (j + 1) * VID] = s
        part = jnp.maximum(s[:, 0:HD], s[:, HD:])
        top = part if top is None else jnp.maximum(top, part)
    return top


def weigh(s, top, v, ones):
    p = jnp.exp2((s - top) * C2).astype(BF16)
    v = jnp.concatenate([v, ones[0 : v.shape[0]]], axis=1)
    return jnp.dot(p, v, preferred_element_type=F32)


def early_body(*refs):
    n = (len(refs) - EARLY - 1) // 3
    q_refs, k_refs = refs[0:n], refs[n : n + EARLY]
    outs, s_ref = refs[n + EARLY : -1], refs[-1]
    k_times = [times_of(k_ref, 2 * VID + 2 * AUD) for k_ref in k_refs]
    ones = jnp.ones((VID, HD), BF16)

    def start(i, h):
        q_ref = q_refs[i]
        cols = slice(h * HD, (h + 1) * HD)
        column = side_by_side(column_times(q_ref)[VID : VID + AUD])
        near_audio = [jnp.abs(column - t[:, 0:VID]) <= WIN for t in k_times]
        top = scores(q_ref[0 : VID + AUD, cols], k_refs, cols, near_audio, s_ref, (i * HPG + h) % 3)
        return jnp.max(top, axis=1, keepdims=True)

    def end(i, h, top):
        cols = slice(h * HD, (h + 1) * HD)
        acc = 0.0
        for j, k_ref in enumerate(k_refs):
            s = s_ref[(i * HPG + h) % 3, :, j * VID : (j + 1) * VID]
            acc = acc + weigh(s, top, k_ref[VID : 2 * VID, cols], ones)
        total = acc[:, HD:]
        outs[2 * i][:, cols] = acc[:, 0:HD] / total
        outs[2 * i + 1][:, cols] = top * C2 + jnp.log2(total)

    work = [(i, h) for i in range(n) for h in range(HPG)]
    tops = {}
    for m, item in enumerate(work):
        tops[item] = start(*item)
        if m >= 2:
            end(*work[m - 2], tops[work[m - 2]])
    for item in work[-2:]:
        end(*item, tops[item])


def early(qs, kvs):
    n, rows, nk = len(qs), VID + AUD, EARLY * VID
    area = n * rows * nk * HPG
    return pl.pallas_call(
        early_body,
        out_shape=tuple(jax.ShapeDtypeStruct((rows, GW), F32) for _ in range(2 * n)),
        in_specs=[VMEM] * (n + EARLY),
        out_specs=tuple(VMEM for _ in range(2 * n)),
        scratch_shapes=[pltpu.VMEM((3, rows, nk), F32)],
        compiler_params=pltpu.CompilerParams(vmem_limit_bytes=16 * 2**20),
        cost_estimate=pl.CostEstimate(flops=6 * area * HD, bytes_accessed=4 << 20, transcendentals=area),
        name="early",
    )(*qs, *kvs)


def late_body(q_ref, o_ref, l_ref, *refs):
    out, s_ref, far_ref, twin_ref = refs[EARLY + 4 :]
    rows = VID + AUD
    for n, ref in enumerate((far_ref, twin_ref)):
        ref[0:VID, :] = refs[EARLY + 2 * n][...]
        ref[VID:, :] = refs[EARLY + 2 * n + 1][...]
    rest = (far_ref, twin_ref)
    k_refs = refs[0:EARLY] + rest
    ka_times = place([times_of(k_ref, 2 * VID + 2 * AUD)[:, VID:] for k_ref in k_refs])
    k_times = [times_of(k_ref, 2 * VID + 2 * AUD) for k_ref in rest]
    column = column_times(q_ref)
    near_video = jnp.abs(column[0:VID] - ka_times) <= WIN
    column = side_by_side(column[VID:rows])
    near_audio = [jnp.abs(column - t[:, 0:VID]) <= WIN for t in k_times]
    ones = jnp.ones((VID, HD), BF16)
    eye = lax.broadcasted_iota(jnp.int32, (HD, HD), 0) == lax.broadcasted_iota(jnp.int32, (HD, HD), 1)
    which = lax.broadcasted_iota(jnp.int32, (AUX, GW), 0)
    first = len(rest) * VID

    def start(h):
        cols = slice(h * HD, (h + 1) * HD)
        q = q_ref[0:rows, cols]
        top = scores(q, rest, cols, near_audio, s_ref, h)
        s = dot_nt(q, jnp.concatenate([k[2 * VID : 2 * VID + AUD, cols] for k in k_refs], axis=0))
        s = jnp.concatenate([jnp.where(near_video, s[0:VID], NEG), s[VID:]], axis=0)
        s_ref[h, :, first:] = s
        return jnp.max(jnp.maximum(top, s), axis=1, keepdims=True)

    def end(h, top):
        cols = slice(h * HD, (h + 1) * HD)
        at = 2 * VID + AUD
        acc = weigh(s_ref[h, :, first:], top, jnp.concatenate([k[at : at + AUD, cols] for k in k_refs], axis=0), ones)
        for j, k_ref in enumerate(rest):
            acc = acc + weigh(s_ref[h, :, j * VID : (j + 1) * VID], top, k_ref[VID : 2 * VID, cols], ones)
        base = top * C2
        before = l_ref[:, cols]
        most = jnp.maximum(base, before)
        w_here, w_before = jnp.exp2(base - most), jnp.exp2(before - most)
        total = acc[:, HD:] * w_here + w_before
        out[0:rows, cols] = ((acc[:, 0:HD] * w_here + o_ref[:, cols] * w_before) / total).astype(BF16)
        lse = most + jnp.log2(total)
        row = jnp.concatenate(
            [
                jnp.sum(jnp.where(eye[0:n], lse[a : a + n], 0.0), axis=0, keepdims=True)
                for a, n in ((0, HD), (HD, HD), (VID, AUD))
            ],
            axis=1,
        )
        hi = row.astype(BF16).astype(F32)
        mid = (row - hi).astype(BF16).astype(F32)
        low = row - hi - mid
        return jnp.where(which == 3 * h, hi, jnp.where(which == 3 * h + 1, mid, jnp.where(which == 3 * h + 2, low, 0.0)))

    tops = [start(h) for h in range(HPG)]
    out[rows:, :] = sum(end(h, tops[h]) for h in range(HPG)).astype(BF16)


def late(q, state, kvs):
    rows, nk = VID + AUD, (NKB - EARLY) * VID + NKB * AUD
    area = rows * nk * HPG
    return pl.pallas_call(
        late_body,
        out_shape=jax.ShapeDtypeStruct((QROWS, GW), BF16),
        in_specs=[VMEM] * (3 + EARLY + 4),
        out_specs=VMEM,
        scratch_shapes=[
            pltpu.VMEM((HPG, rows, nk), F32),
            pltpu.VMEM((KROWS, GW), BF16),
            pltpu.VMEM((KROWS, GW), BF16),
        ],
        compiler_params=pltpu.CompilerParams(vmem_limit_bytes=16 * 2**20),
        cost_estimate=pl.CostEstimate(flops=6 * area * HD, bytes_accessed=5 << 20, transcendentals=area),
        name="late",
    )(q, *state, *kvs)


def combine_body(a_ref, b_ref, c_ref, d_ref, video_out, audio_out):
    refs = (a_ref, b_ref, c_ref, d_ref)
    rows = VID + AUD
    which = lax.broadcasted_iota(jnp.int32, (AUX, HD), 0)
    for h in range(HPG):
        pick = jnp.where((which >= 3 * h) & (which < 3 * h + 3), 1.0, 0.0).astype(BF16)
        lses = [dot_tn(ref[rows:, :], pick)[0:rows] for ref in refs]
        top = functools.reduce(jnp.maximum, lses)
        weights = [jnp.exp2(x - top) for x in lses]
        scale = 1.0 / sum(weights)
        cols = slice(h * HD, (h + 1) * HD)
        out = sum(ref[0:rows, cols].astype(F32) * (w * scale) for ref, w in zip(refs, weights, strict=True))
        out = out.astype(BF16)
        for g in range(NZ):
            video_out[g, :, cols] = out[g * TOK : (g + 1) * TOK]
        audio_out[:, cols] = out[VID:]


def combine(parts):
    return pl.pallas_call(
        combine_body,
        out_shape=(
            jax.ShapeDtypeStruct((NZ, TOK, GW), BF16),
            jax.ShapeDtypeStruct((AUD, GW), BF16),
        ),
        in_specs=[VMEM] * NX,
        out_specs=(VMEM, VMEM),
        compiler_params=SMALL,
        name="combine",
    )(*parts)


def spread_body(video_ref, audio_ref, video_out, audio_out, rows_ref, sems):
    audio_copy = pltpu.make_async_copy(audio_ref, audio_out, sems.at[0])
    audio_copy.start()
    for g in range(NZ):
        rows_ref[:, g * GW : (g + 1) * GW] = video_ref[g]
    video_copy = pltpu.make_async_copy(rows_ref, video_out, sems.at[1])
    video_copy.start()
    audio_copy.wait()
    video_copy.wait()


def spread(video, audio):
    return pl.pallas_call(
        spread_body,
        out_shape=(
            jax.ShapeDtypeStruct((TOK, NZ * GW), BF16),
            jax.ShapeDtypeStruct((AUD, GW), BF16),
        ),
        in_specs=[VMEM, VMEM],
        out_specs=(ANY, ANY),
        scratch_shapes=[pltpu.VMEM((TOK, NZ * GW), BF16), pltpu.SemaphoreType.DMA((2,))],
        compiler_params=SMALL,
        name="spread",
    )(video, audio)


def shift(x, axis, n, k):
    return lax.ppermute(x, axis, [(i, (i + k) % n) for i in range(n)])


PLACES = ((2, 1), (1, 1), (2, 0), (1, 0), (0, 0), (3, 0), (0, 1), (3, 1))


def audio_pairs():
    pairs = []
    for group in range(NZ):
        for ahead, (dx, dy) in enumerate(PLACES):
            there = ((group // 2 + dx) % NX) * 2 + (group % 2 + dy) % 2
            pairs.append((group * NZ + (group + ahead) % NZ, there * NZ + group))
    return pairs


def audio_z():
    group = lax.axis_index("z")
    dx = lax.rem(lax.axis_index("x") + NX - group // 2, NX)
    dy = lax.rem(lax.axis_index("yh") + 2 - lax.rem(group, 2), 2)
    ahead = 0
    for n, (px, py) in enumerate(PLACES):
        ahead = jnp.where((dx == px) & (dy == py), n, ahead)
    return lax.rem(group + ahead, NZ)


def to_group(x):
    return lax.ppermute(x, ("x", "yh", "z"), audio_pairs())


def from_group(x):
    return lax.ppermute(x, ("x", "yh", "z"), [(b, a) for a, b in audio_pairs()])


def on_device(video_q, video_k, video_v, audio_q, audio_k, audio_v, align):
    aud = to_group(jnp.concatenate([audio_q, audio_k, audio_v], axis=1))
    got = lax.all_to_all(
        pack(align, video_q, video_k, video_v), "z", split_axis=0, concat_axis=0, tiled=True
    )
    q_own, kv_own = join(got, aud)
    y = ("yh", "yl")
    core = functools.partial(shift, axis="c", n=NC, k=1)
    right, left = [shift(kv_own, y, NY, k) for k in (1, 3)]
    q_right, q_left = [shift(q_own, "x", NX, k) for k in (1, 3)]
    got = lax.optimization_barrier([left, right, q_left, q_right, q_own, kv_own])
    left, right, q_left, q_right, q_own, kv_own = got
    far = [shift(right[0:VID], y, NY, 1), shift(left[VID:], y, NY, 3)]
    q_far = shift(q_right, "x", NX, 1)
    kvs = [kv_own, right, left] + [core(b) for b in (kv_own, right, left)]
    state = early([q_right, q_left, q_own], kvs)
    far, q_far, state = lax.optimization_barrier((far, q_far, state))
    others = [core(b) for b in far]
    state_far = early([q_far], kvs)
    kvs = kvs + far + others
    part_far, state = lax.optimization_barrier((late(q_far, state_far, kvs), state))
    parts = [part_far] + [late(q, state[2 * i : 2 * i + 2], kvs) for i, q in enumerate([q_right, q_left, q_own])]
    back = [shift(p, "x", NX, -k) for p, k in zip(parts, (2, 1, 3))]
    video, audio = combine(parts[3:] + back)
    video = lax.all_to_all(video, "z", split_axis=0, concat_axis=0, tiled=True)
    return spread(video, from_group(audio))


def solution(mesh):
    grid = Mesh(np.asarray(mesh.devices).reshape(4, 2, 2, 8, 2), ("x", "yh", "yl", "z", "c"))
    seq, head = ("yl", "z", "c"), ("x", "yh")
    rows = P(seq + head, None)
    audio = P(seq, head)
    return jax.shard_map(
        on_device,
        mesh=grid,
        in_specs=(rows, rows, rows, audio, audio, audio, P(seq + head)),
        out_specs=(rows, audio),
        check_vma=False,
    )
```

```python
import functools

import jax
import jax.numpy as jnp
import numpy as np
from jax import lax
from jax.experimental import pallas as pl
from jax.experimental.pallas import tpu as pltpu
from jax.sharding import Mesh
from jax.sharding import PartitionSpec as P

HD = 128
HPG = 3
GW = HPG * HD
NZ, NX, NY, NC = 8, 4, 4, 2
TOK = 32
AUD = 16
VID = NZ * TOK
STAMPS = 8
AUX = 16
QROWS = VID + AUD + AUX
KROWS = 2 * VID + 2 * AUD + AUX
NKB = NY * NC
EARLY = 6
WIN = 64.0
NEG = -1e30
C2 = HD**-0.5 * 1.4426950408889634
F32, BF16 = jnp.float32, jnp.bfloat16
VMEM = pl.BlockSpec(memory_space=pltpu.VMEM)
SMEM = pl.BlockSpec(memory_space=pltpu.SMEM)
ANY = pl.BlockSpec(memory_space=pl.ANY)
SMALL = pltpu.CompilerParams(vmem_limit_bytes=6 * 2**20)


def pack_body(align_ref, q_ref, k_ref, v_ref, out):
    first = lax.axis_index("z") * TOK
    lane = lax.broadcasted_iota(jnp.int32, (1, GW), 1)
    row = jnp.zeros((1, GW), jnp.int32)
    for i in range(TOK):
        row = jnp.where(lane == first + i, align_ref[i], row)
    high = (row >> 4).astype(F32)
    low = (row & 15).astype(F32)
    which = lax.broadcasted_iota(jnp.int32, (STAMPS, GW), 0)
    stamps = jnp.where(which == 0, high, jnp.where(which == 1, low, 0.0)).astype(BF16)
    for g in range(NZ):
        cols = slice(g * GW, (g + 1) * GW)
        out[g, 0:TOK, :] = q_ref[:, cols]
        out[g, TOK : 2 * TOK, :] = k_ref[:, cols]
        out[g, 2 * TOK : 3 * TOK, :] = v_ref[:, cols]
        out[g, 3 * TOK :, :] = stamps


def pack(align, q, k, v):
    return pl.pallas_call(
        pack_body,
        out_shape=jax.ShapeDtypeStruct((NZ, 3 * TOK + STAMPS, GW), BF16),
        in_specs=[SMEM, VMEM, VMEM, VMEM],
        out_specs=VMEM,
        name="pack",
    )(align, q, k, v)


def audio_times(start):
    lane = lax.broadcasted_iota(jnp.int32, (STAMPS, GW), 1) - VID
    which = lax.broadcasted_iota(jnp.int32, (STAMPS, GW), 0)
    stamp = lane + start
    here = (lane >= 0) & (lane < AUD)
    part = jnp.where(which == 0, stamp >> 4, jnp.where(which == 1, stamp & 15, 0))
    return jnp.where(here, part, 0).astype(F32)


def join_body(got_ref, aud_ref, q_out, kv_out):
    block = lax.axis_index("yl") * 16 + audio_z() * 2 + lax.axis_index("c")
    total = audio_times(block * AUD)
    for g in range(NZ):
        at = g * TOK
        q_out[at : at + TOK, :] = got_ref[g, 0:TOK, :]
        kv_out[at : at + TOK, :] = got_ref[g, TOK : 2 * TOK, :]
        kv_out[VID + at : VID + at + TOK, :] = got_ref[g, 2 * TOK : 3 * TOK, :]
        total = total + got_ref[g, 3 * TOK :, :].astype(F32)
    total = jnp.concatenate([total, jnp.zeros((AUX - STAMPS, GW), F32)], axis=0)
    q_out[VID : VID + AUD, :] = aud_ref[:, 0:GW]
    kv_out[2 * VID : 2 * VID + AUD, :] = aud_ref[:, GW : 2 * GW]
    kv_out[2 * VID + AUD : 2 * VID + 2 * AUD, :] = aud_ref[:, 2 * GW :]
    q_out[VID + AUD :, :] = total.astype(BF16)
    kv_out[2 * VID + 2 * AUD :, :] = total.astype(BF16)


def join(got, aud):
    return pl.pallas_call(
        join_body,
        out_shape=(
            pltpu.VMEM((QROWS, GW), BF16),
            pltpu.VMEM((KROWS, GW), BF16),
        ),
        in_specs=[VMEM, VMEM],
        out_specs=(VMEM, VMEM),
        compiler_params=SMALL,
        name="join",
    )(got, aud)


def place(rows):
    return sum(
        pltpu.roll(jnp.broadcast_to(row, (8, HD)), i * AUD, 1) if i else jnp.broadcast_to(row, (8, HD))
        for i, row in enumerate(rows)
    )[0:1, :]


def dot_nt(a, b):
    return lax.dot_general(a, b, (((1,), (1,)), ((), ())), preferred_element_type=F32)


def dot_tn(a, b):
    return lax.dot_general(a, b, (((0,), (0,)), ((), ())), preferred_element_type=F32)


def times_of(ref, first):
    aux = ref[first : first + AUX, :].astype(F32)
    return aux[0:1, :] * 16.0 + aux[1:2, :]


def column_times(q_ref):
    which = lax.broadcasted_iota(jnp.int32, (AUX, HD), 0)
    pick = jnp.where(which == 0, 16.0, jnp.where(which == 1, 1.0, 0.0)).astype(BF16)
    return dot_tn(q_ref[VID + AUD : QROWS, :], pick)


def side_by_side(x):
    return jnp.concatenate([x, x], axis=1)


def scores(q, k_refs, cols, near_audio, s_ref, h):
    top = None
    for j, k_ref in enumerate(k_refs):
        s = dot_nt(q, k_ref[0:VID, cols])
        s = jnp.concatenate([s[0:VID], jnp.where(near_audio[j], s[VID:], NEG)], axis=0)
        s_ref[h, :, j * VID : (j + 1) * VID] = s
        part = jnp.maximum(s[:, 0:HD], s[:, HD:])
        top = part if top is None else jnp.maximum(top, part)
    return top


def weigh(s, top, v, ones):
    p = jnp.exp2((s - top) * C2).astype(BF16)
    v = jnp.concatenate([v, ones[0 : v.shape[0]]], axis=1)
    return jnp.dot(p, v, preferred_element_type=F32)


def early_body(*refs):
    n = (len(refs) - EARLY - 1) // 3
    q_refs, k_refs = refs[0:n], refs[n : n + EARLY]
    outs, s_ref = refs[n + EARLY : -1], refs[-1]
    k_times = [times_of(k_ref, 2 * VID + 2 * AUD) for k_ref in k_refs]
    ones = jnp.ones((VID, HD), BF16)

    def start(i, h):
        q_ref = q_refs[i]
        cols = slice(h * HD, (h + 1) * HD)
        column = side_by_side(column_times(q_ref)[VID : VID + AUD])
        near_audio = [jnp.abs(column - t[:, 0:VID]) <= WIN for t in k_times]
        top = scores(q_ref[0 : VID + AUD, cols], k_refs, cols, near_audio, s_ref, (i * HPG + h) % 3)
        return jnp.max(top, axis=1, keepdims=True)

    def end(i, h, top):
        cols = slice(h * HD, (h + 1) * HD)
        acc = 0.0
        for j, k_ref in enumerate(k_refs):
            s = s_ref[(i * HPG + h) % 3, :, j * VID : (j + 1) * VID]
            acc = acc + weigh(s, top, k_ref[VID : 2 * VID, cols], ones)
        total = acc[:, HD:]
        outs[2 * i][:, cols] = acc[:, 0:HD] / total
        outs[2 * i + 1][:, cols] = top * C2 + jnp.log2(total)

    work = [(i, h) for i in range(n) for h in range(HPG)]
    tops = {}
    for m, item in enumerate(work):
        tops[item] = start(*item)
        if m >= 2:
            end(*work[m - 2], tops[work[m - 2]])
    for item in work[-2:]:
        end(*item, tops[item])


def early(qs, kvs):
    n, rows, nk = len(qs), VID + AUD, EARLY * VID
    area = n * rows * nk * HPG
    return pl.pallas_call(
        early_body,
        out_shape=tuple(jax.ShapeDtypeStruct((rows, GW), F32) for _ in range(2 * n)),
        in_specs=[VMEM] * (n + EARLY),
        out_specs=tuple(VMEM for _ in range(2 * n)),
        scratch_shapes=[pltpu.VMEM((3, rows, nk), F32)],
        compiler_params=pltpu.CompilerParams(vmem_limit_bytes=16 * 2**20),
        cost_estimate=pl.CostEstimate(flops=6 * area * HD, bytes_accessed=4 << 20, transcendentals=area),
        name="early",
    )(*qs, *kvs)


def late_body(q_ref, o_ref, l_ref, *refs):
    out, s_ref, far_ref, twin_ref = refs[EARLY + 4 :]
    rows = VID + AUD
    for n, ref in enumerate((far_ref, twin_ref)):
        ref[0:VID, :] = refs[EARLY + 2 * n][...]
        ref[VID:, :] = refs[EARLY + 2 * n + 1][...]
    rest = (far_ref, twin_ref)
    k_refs = refs[0:EARLY] + rest
    ka_times = place([times_of(k_ref, 2 * VID + 2 * AUD)[:, VID:] for k_ref in k_refs])
    k_times = [times_of(k_ref, 2 * VID + 2 * AUD) for k_ref in rest]
    column = column_times(q_ref)
    near_video = jnp.abs(column[0:VID] - ka_times) <= WIN
    column = side_by_side(column[VID:rows])
    near_audio = [jnp.abs(column - t[:, 0:VID]) <= WIN for t in k_times]
    ones = jnp.ones((VID, HD), BF16)
    eye = lax.broadcasted_iota(jnp.int32, (HD, HD), 0) == lax.broadcasted_iota(jnp.int32, (HD, HD), 1)
    which = lax.broadcasted_iota(jnp.int32, (AUX, GW), 0)
    first = len(rest) * VID

    def start(h):
        cols = slice(h * HD, (h + 1) * HD)
        q = q_ref[0:rows, cols]
        top = scores(q, rest, cols, near_audio, s_ref, h)
        s = dot_nt(q, jnp.concatenate([k[2 * VID : 2 * VID + AUD, cols] for k in k_refs], axis=0))
        s = jnp.concatenate([jnp.where(near_video, s[0:VID], NEG), s[VID:]], axis=0)
        s_ref[h, :, first:] = s
        return jnp.max(jnp.maximum(top, s), axis=1, keepdims=True)

    def end(h, top):
        cols = slice(h * HD, (h + 1) * HD)
        at = 2 * VID + AUD
        acc = weigh(s_ref[h, :, first:], top, jnp.concatenate([k[at : at + AUD, cols] for k in k_refs], axis=0), ones)
        for j, k_ref in enumerate(rest):
            acc = acc + weigh(s_ref[h, :, j * VID : (j + 1) * VID], top, k_ref[VID : 2 * VID, cols], ones)
        base = top * C2
        before = l_ref[:, cols]
        most = jnp.maximum(base, before)
        w_here, w_before = jnp.exp2(base - most), jnp.exp2(before - most)
        total = acc[:, HD:] * w_here + w_before
        out[0:rows, cols] = ((acc[:, 0:HD] * w_here + o_ref[:, cols] * w_before) / total).astype(BF16)
        lse = most + jnp.log2(total)
        row = jnp.concatenate(
            [
                jnp.sum(jnp.where(eye[0:n], lse[a : a + n], 0.0), axis=0, keepdims=True)
                for a, n in ((0, HD), (HD, HD), (VID, AUD))
            ],
            axis=1,
        )
        hi = row.astype(BF16).astype(F32)
        mid = (row - hi).astype(BF16).astype(F32)
        low = row - hi - mid
        return jnp.where(which == 3 * h, hi, jnp.where(which == 3 * h + 1, mid, jnp.where(which == 3 * h + 2, low, 0.0)))

    tops = [start(h) for h in range(HPG)]
    out[rows:, :] = sum(end(h, tops[h]) for h in range(HPG)).astype(BF16)


def late(q, state, kvs):
    rows, nk = VID + AUD, (NKB - EARLY) * VID + NKB * AUD
    area = rows * nk * HPG
    return pl.pallas_call(
        late_body,
        out_shape=jax.ShapeDtypeStruct((QROWS, GW), BF16),
        in_specs=[VMEM] * (3 + EARLY + 4),
        out_specs=VMEM,
        scratch_shapes=[
            pltpu.VMEM((HPG, rows, nk), F32),
            pltpu.VMEM((KROWS, GW), BF16),
            pltpu.VMEM((KROWS, GW), BF16),
        ],
        compiler_params=pltpu.CompilerParams(vmem_limit_bytes=16 * 2**20),
        cost_estimate=pl.CostEstimate(flops=6 * area * HD, bytes_accessed=5 << 20, transcendentals=area),
        name="late",
    )(q, *state, *kvs)


def combine_body(a_ref, b_ref, c_ref, d_ref, video_out, audio_out):
    refs = (a_ref, b_ref, c_ref, d_ref)
    rows = VID + AUD
    auxes = [ref[rows:, :].astype(F32) for ref in refs]
    which = lax.broadcasted_iota(jnp.int32, (2 * AUX, GW), 0)
    table = jnp.zeros((2 * AUX, GW), F32)
    for h in range(HPG):
        lses = [x[3 * h : 3 * h + 1] + x[3 * h + 1 : 3 * h + 2] + x[3 * h + 2 : 3 * h + 3] for x in auxes]
        top = functools.reduce(jnp.maximum, lses)
        weights = [jnp.exp2(x - top) for x in lses]
        scale = 1.0 / sum(weights)
        for i, w in enumerate(weights):
            w = w * scale
            hi = w.astype(BF16).astype(F32)
            at = 2 * (NX * h + i)
            table = jnp.where(which == at, hi, jnp.where(which == at + 1, w - hi, table))
    table = table.astype(BF16)
    which = lax.broadcasted_iota(jnp.int32, (2 * AUX, HD), 0)
    for h in range(HPG):
        cols = slice(h * HD, (h + 1) * HD)
        out = 0.0
        for i, ref in enumerate(refs):
            at = 2 * (NX * h + i)
            pick = jnp.where((which == at) | (which == at + 1), 1.0, 0.0).astype(BF16)
            out = out + ref[0:rows, cols].astype(F32) * dot_tn(table, pick)[0:rows]
        out = out.astype(BF16)
        for g in range(NZ):
            video_out[g, :, cols] = out[g * TOK : (g + 1) * TOK]
        audio_out[:, cols] = out[VID:]


def combine(parts):
    return pl.pallas_call(
        combine_body,
        out_shape=(
            jax.ShapeDtypeStruct((NZ, TOK, GW), BF16),
            jax.ShapeDtypeStruct((AUD, GW), BF16),
        ),
        in_specs=[VMEM] * NX,
        out_specs=(VMEM, VMEM),
        compiler_params=SMALL,
        name="combine",
    )(*parts)


def spread_body(video_ref, audio_ref, video_out, audio_out, rows_ref, sems):
    audio_copy = pltpu.make_async_copy(audio_ref, audio_out, sems.at[0])
    audio_copy.start()
    for g in range(NZ):
        rows_ref[:, g * GW : (g + 1) * GW] = video_ref[g]
    video_copy = pltpu.make_async_copy(rows_ref, video_out, sems.at[1])
    video_copy.start()
    audio_copy.wait()
    video_copy.wait()


def spread(video, audio):
    return pl.pallas_call(
        spread_body,
        out_shape=(
            jax.ShapeDtypeStruct((TOK, NZ * GW), BF16),
            jax.ShapeDtypeStruct((AUD, GW), BF16),
        ),
        in_specs=[VMEM, VMEM],
        out_specs=(ANY, ANY),
        scratch_shapes=[pltpu.VMEM((TOK, NZ * GW), BF16), pltpu.SemaphoreType.DMA((2,))],
        compiler_params=SMALL,
        name="spread",
    )(video, audio)


def shift(x, axis, n, k):
    return lax.ppermute(x, axis, [(i, (i + k) % n) for i in range(n)])


PLACES = ((2, 1), (1, 1), (2, 0), (1, 0), (0, 0), (3, 0), (0, 1), (3, 1))


def audio_pairs():
    pairs = []
    for group in range(NZ):
        for ahead, (dx, dy) in enumerate(PLACES):
            there = ((group // 2 + dx) % NX) * 2 + (group % 2 + dy) % 2
            pairs.append((group * NZ + (group + ahead) % NZ, there * NZ + group))
    return pairs


def audio_z():
    group = lax.axis_index("z")
    dx = lax.rem(lax.axis_index("x") + NX - group // 2, NX)
    dy = lax.rem(lax.axis_index("yh") + 2 - lax.rem(group, 2), 2)
    ahead = 0
    for n, (px, py) in enumerate(PLACES):
        ahead = jnp.where((dx == px) & (dy == py), n, ahead)
    return lax.rem(group + ahead, NZ)


def to_group(x):
    return lax.ppermute(x, ("x", "yh", "z"), audio_pairs())


def from_group(x):
    return lax.ppermute(x, ("x", "yh", "z"), [(b, a) for a, b in audio_pairs()])


def on_device(video_q, video_k, video_v, audio_q, audio_k, audio_v, align):
    aud = to_group(jnp.concatenate([audio_q, audio_k, audio_v], axis=1))
    got = lax.all_to_all(
        pack(align, video_q, video_k, video_v), "z", split_axis=0, concat_axis=0, tiled=True
    )
    q_own, kv_own = join(got, aud)
    y = ("yh", "yl")
    core = functools.partial(shift, axis="c", n=NC, k=1)
    right, left = [shift(kv_own, y, NY, k) for k in (1, 3)]
    q_right, q_left = [shift(q_own, "x", NX, k) for k in (1, 3)]
    q_far = shift(q_right, "x", NX, 1)
    got = lax.optimization_barrier([left, right, q_left, q_right, q_own, kv_own])
    left, right, q_left, q_right, q_own, kv_own = got
    far = [shift(right[0:VID], y, NY, 1), shift(left[VID:], y, NY, 3)]
    kvs = [kv_own, right, left] + [core(b) for b in (kv_own, right, left)]
    state = early([q_right, q_left, q_own], kvs)
    far, q_far, state = lax.optimization_barrier((far, q_far, state))
    others = [core(b) for b in far]
    state_far = early([q_far], kvs)
    kvs = kvs + far + others
    part_far, state = lax.optimization_barrier((late(q_far, state_far, kvs), state))
    parts = [part_far] + [late(q, state[2 * i : 2 * i + 2], kvs) for i, q in enumerate([q_right, q_left, q_own])]
    back = [shift(p, "x", NX, -k) for p, k in zip(parts, (2, 1, 3))]
    video, audio = combine(parts[3:] + back)
    video = lax.all_to_all(video, "z", split_axis=0, concat_axis=0, tiled=True)
    return spread(video, from_group(audio))


def solution(mesh):
    grid = Mesh(np.asarray(mesh.devices).reshape(4, 2, 2, 8, 2), ("x", "yh", "yl", "z", "c"))
    seq, head = ("yl", "z", "c"), ("x", "yh")
    rows = P(seq + head, None)
    audio = P(seq, head)
    return jax.shard_map(
        on_device,
        mesh=grid,
        in_specs=(rows, rows, rows, audio, audio, audio, P(seq + head)),
        out_specs=(rows, audio),
        check_vma=False,
    )
```

```python
import functools

import jax
import jax.numpy as jnp
import numpy as np
from jax import lax
from jax.experimental import pallas as pl
from jax.experimental.pallas import tpu as pltpu
from jax.sharding import Mesh
from jax.sharding import PartitionSpec as P

HD = 128
HPG = 3
GW = HPG * HD
NZ, NX, NY, NC = 8, 4, 4, 2
TOK = 32
AUD = 16
VID = NZ * TOK
STAMPS = 8
AUX = 16
QROWS = VID + AUD + AUX
KROWS = 2 * VID + 2 * AUD + AUX
NKB = NY * NC
EARLY = 6
WIN = 64.0
NEG = -1e30
C2 = HD**-0.5 * 1.4426950408889634
F32, BF16 = jnp.float32, jnp.bfloat16
VMEM = pl.BlockSpec(memory_space=pltpu.VMEM)
SMEM = pl.BlockSpec(memory_space=pltpu.SMEM)
ANY = pl.BlockSpec(memory_space=pl.ANY)
SMALL = pltpu.CompilerParams(vmem_limit_bytes=6 * 2**20)


def pack_body(align_ref, q_ref, k_ref, v_ref, out):
    first = lax.axis_index("z") * TOK
    lane = lax.broadcasted_iota(jnp.int32, (1, GW), 1)
    row = jnp.zeros((1, GW), jnp.int32)
    for i in range(TOK):
        row = jnp.where(lane == first + i, align_ref[i], row)
    high = (row >> 4).astype(F32)
    low = (row & 15).astype(F32)
    which = lax.broadcasted_iota(jnp.int32, (STAMPS, HD), 0)
    stamps = jnp.zeros((STAMPS, HD), F32)
    for n, part in enumerate((high[:, 0:HD], high[:, HD:VID], low[:, 0:HD], low[:, HD:VID])):
        stamps = jnp.where(which == n, part, stamps)
    stamps = stamps.astype(BF16)
    for g in range(NZ):
        for n, ref in enumerate((q_ref, k_ref, v_ref)):
            for h in range(HPG):
                at = (n * HPG + h) * TOK
                out[g, at : at + TOK, :] = ref[:, (g * HPG + h) * HD : (g * HPG + h + 1) * HD]
        out[g, 3 * HPG * TOK :, :] = stamps


def pack(align, q, k, v):
    return pl.pallas_call(
        pack_body,
        out_shape=jax.ShapeDtypeStruct((NZ, 3 * HPG * TOK + STAMPS, HD), BF16),
        in_specs=[SMEM, VMEM, VMEM, VMEM],
        out_specs=VMEM,
        name="pack",
    )(align, q, k, v)


def audio_times(start):
    lane = lax.broadcasted_iota(jnp.int32, (AUX, GW), 1) - VID
    which = lax.broadcasted_iota(jnp.int32, (AUX, GW), 0)
    stamp = lane + start
    here = (lane >= 0) & (lane < AUD)
    part = jnp.where(which == 0, stamp >> 4, jnp.where(which == 1, stamp & 15, 0))
    return jnp.where(here, part, 0).astype(F32)


def join_body(got_ref, aud_ref, q_out, kv_out):
    block = lax.axis_index("yl") * 16 + audio_z() * 2 + lax.axis_index("c")
    stamps = jnp.zeros((STAMPS, HD), F32)
    for g in range(NZ):
        for h in range(HPG):
            cols = slice(h * HD, (h + 1) * HD)
            for n, (out, first) in enumerate(((q_out, 0), (kv_out, 0), (kv_out, VID))):
                at = (n * HPG + h) * TOK
                out[first + g * TOK : first + (g + 1) * TOK, cols] = got_ref[g, at : at + TOK, :]
        stamps = stamps + got_ref[g, 3 * HPG * TOK :, :].astype(F32)
    none = jnp.zeros((1, HD), F32)
    high = jnp.concatenate([stamps[0:1], stamps[1:2], none], axis=1)
    low = jnp.concatenate([stamps[2:3], stamps[3:4], none], axis=1)
    which = lax.broadcasted_iota(jnp.int32, (AUX, GW), 0)
    aux = jnp.where(which == 0, high, jnp.where(which == 1, low, 0.0)) + audio_times(block * AUD)
    aux = aux.astype(BF16)
    q_out[VID : VID + AUD, :] = aud_ref[:, 0:GW]
    kv_out[2 * VID : 2 * VID + AUD, :] = aud_ref[:, GW : 2 * GW]
    kv_out[2 * VID + AUD : 2 * VID + 2 * AUD, :] = aud_ref[:, 2 * GW :]
    q_out[VID + AUD :, :] = aux
    kv_out[2 * VID + 2 * AUD :, :] = aux


def join(got, aud):
    return pl.pallas_call(
        join_body,
        out_shape=(
            pltpu.VMEM((QROWS, GW), BF16),
            pltpu.VMEM((KROWS, GW), BF16),
        ),
        in_specs=[VMEM, VMEM],
        out_specs=(VMEM, VMEM),
        compiler_params=SMALL,
        name="join",
    )(got, aud)


def place(rows):
    return sum(
        pltpu.roll(jnp.broadcast_to(row, (8, HD)), i * AUD, 1) if i else jnp.broadcast_to(row, (8, HD))
        for i, row in enumerate(rows)
    )[0:1, :]


def dot_nt(a, b):
    return lax.dot_general(a, b, (((1,), (1,)), ((), ())), preferred_element_type=F32)


def dot_tn(a, b):
    return lax.dot_general(a, b, (((0,), (0,)), ((), ())), preferred_element_type=F32)


def times_of(ref, first):
    aux = ref[first : first + AUX, :].astype(F32)
    return aux[0:1, :] * 16.0 + aux[1:2, :]


def column_times(q_ref):
    which = lax.broadcasted_iota(jnp.int32, (AUX, HD), 0)
    pick = jnp.where(which == 0, 16.0, jnp.where(which == 1, 1.0, 0.0)).astype(BF16)
    return dot_tn(q_ref[VID + AUD : QROWS, :], pick)


def side_by_side(x):
    return jnp.concatenate([x, x], axis=1)


def scores(q, k_refs, cols, near_audio, s_ref, h):
    top = None
    for j, k_ref in enumerate(k_refs):
        s = dot_nt(q, k_ref[0:VID, cols])
        s = jnp.concatenate([s[0:VID], jnp.where(near_audio[j], s[VID:], NEG)], axis=0)
        s_ref[h, :, j * VID : (j + 1) * VID] = s
        part = jnp.maximum(s[:, 0:HD], s[:, HD:])
        top = part if top is None else jnp.maximum(top, part)
    return top


def weigh(s, top, v, ones):
    p = jnp.exp2((s - top) * C2).astype(BF16)
    v = jnp.concatenate([v, ones[0 : v.shape[0]]], axis=1)
    return jnp.dot(p, v, preferred_element_type=F32)


def early_body(*refs):
    n = (len(refs) - EARLY - 1) // 3
    q_refs, k_refs = refs[0:n], refs[n : n + EARLY]
    outs, s_ref = refs[n + EARLY : -1], refs[-1]
    k_times = [times_of(k_ref, 2 * VID + 2 * AUD) for k_ref in k_refs]
    ones = jnp.ones((VID, HD), BF16)

    def start(i, h):
        q_ref = q_refs[i]
        cols = slice(h * HD, (h + 1) * HD)
        column = side_by_side(column_times(q_ref)[VID : VID + AUD])
        near_audio = [jnp.abs(column - t[:, 0:VID]) <= WIN for t in k_times]
        top = scores(q_ref[0 : VID + AUD, cols], k_refs, cols, near_audio, s_ref, (i * HPG + h) % 3)
        return jnp.max(top, axis=1, keepdims=True)

    def end(i, h, top):
        cols = slice(h * HD, (h + 1) * HD)
        acc = 0.0
        for j, k_ref in enumerate(k_refs):
            s = s_ref[(i * HPG + h) % 3, :, j * VID : (j + 1) * VID]
            acc = acc + weigh(s, top, k_ref[VID : 2 * VID, cols], ones)
        total = acc[:, HD:]
        outs[2 * i][:, cols] = acc[:, 0:HD] / total
        outs[2 * i + 1][:, cols] = top * C2 + jnp.log2(total)

    work = [(i, h) for i in range(n) for h in range(HPG)]
    tops = {}
    for m, item in enumerate(work):
        tops[item] = start(*item)
        if m >= 2:
            end(*work[m - 2], tops[work[m - 2]])
    for item in work[-2:]:
        end(*item, tops[item])


def early(qs, kvs):
    n, rows, nk = len(qs), VID + AUD, EARLY * VID
    area = n * rows * nk * HPG
    return pl.pallas_call(
        early_body,
        out_shape=tuple(jax.ShapeDtypeStruct((rows, GW), F32) for _ in range(2 * n)),
        in_specs=[VMEM] * (n + EARLY),
        out_specs=tuple(VMEM for _ in range(2 * n)),
        scratch_shapes=[pltpu.VMEM((3, rows, nk), F32)],
        compiler_params=pltpu.CompilerParams(vmem_limit_bytes=16 * 2**20),
        cost_estimate=pl.CostEstimate(flops=6 * area * HD, bytes_accessed=4 << 20, transcendentals=area),
        name="early",
    )(*qs, *kvs)


class Block:
    def __init__(self, keys, rest):
        self.keys, self.rest = keys, rest

    def __getitem__(self, at):
        rows, cols = at
        if rows.stop <= VID:
            return self.keys[rows, cols]
        return self.rest[rows.start - VID : rows.stop - VID, cols]


def late_body(q_ref, o_ref, l_ref, *refs):
    out, s_ref = refs[EARLY + 4 :]
    rows = VID + AUD
    rest = (Block(*refs[EARLY : EARLY + 2]), Block(*refs[EARLY + 2 : EARLY + 4]))
    k_refs = refs[0:EARLY] + rest
    ka_times = place([times_of(k_ref, 2 * VID + 2 * AUD)[:, VID:] for k_ref in k_refs])
    k_times = [times_of(k_ref, 2 * VID + 2 * AUD) for k_ref in rest]
    column = column_times(q_ref)
    near_video = jnp.abs(column[0:VID] - ka_times) <= WIN
    column = side_by_side(column[VID:rows])
    near_audio = [jnp.abs(column - t[:, 0:VID]) <= WIN for t in k_times]
    ones = jnp.ones((VID, HD), BF16)
    eye = lax.broadcasted_iota(jnp.int32, (HD, HD), 0) == lax.broadcasted_iota(jnp.int32, (HD, HD), 1)
    which = lax.broadcasted_iota(jnp.int32, (AUX, GW), 0)
    first = len(rest) * VID

    def start(h):
        cols = slice(h * HD, (h + 1) * HD)
        q = q_ref[0:rows, cols]
        top = scores(q, rest, cols, near_audio, s_ref, h)
        s = dot_nt(q, jnp.concatenate([k[2 * VID : 2 * VID + AUD, cols] for k in k_refs], axis=0))
        s = jnp.concatenate([jnp.where(near_video, s[0:VID], NEG), s[VID:]], axis=0)
        s_ref[h, :, first:] = s
        return jnp.max(jnp.maximum(top, s), axis=1, keepdims=True)

    def end(h, top):
        cols = slice(h * HD, (h + 1) * HD)
        at = 2 * VID + AUD
        acc = weigh(s_ref[h, :, first:], top, jnp.concatenate([k[at : at + AUD, cols] for k in k_refs], axis=0), ones)
        for j, k_ref in enumerate(rest):
            acc = acc + weigh(s_ref[h, :, j * VID : (j + 1) * VID], top, k_ref[VID : 2 * VID, cols], ones)
        base = top * C2
        before = l_ref[:, cols]
        most = jnp.maximum(base, before)
        w_here, w_before = jnp.exp2(base - most), jnp.exp2(before - most)
        total = acc[:, HD:] * w_here + w_before
        out[0:rows, cols] = ((acc[:, 0:HD] * w_here + o_ref[:, cols] * w_before) / total).astype(BF16)
        lse = most + jnp.log2(total)
        row = jnp.concatenate(
            [
                jnp.sum(jnp.where(eye[0:n], lse[a : a + n], 0.0), axis=0, keepdims=True)
                for a, n in ((0, HD), (HD, HD), (VID, AUD))
            ],
            axis=1,
        )
        hi = row.astype(BF16).astype(F32)
        mid = (row - hi).astype(BF16).astype(F32)
        low = row - hi - mid
        return jnp.where(which == 3 * h, hi, jnp.where(which == 3 * h + 1, mid, jnp.where(which == 3 * h + 2, low, 0.0)))

    tops = [start(h) for h in range(HPG)]
    out[rows:, :] = sum(end(h, tops[h]) for h in range(HPG)).astype(BF16)


def late(q, state, kvs):
    rows, nk = VID + AUD, (NKB - EARLY) * VID + NKB * AUD
    area = rows * nk * HPG
    return pl.pallas_call(
        late_body,
        out_shape=jax.ShapeDtypeStruct((QROWS, GW), BF16),
        in_specs=[VMEM] * (3 + EARLY + 4),
        out_specs=VMEM,
        scratch_shapes=[pltpu.VMEM((HPG, rows, nk), F32)],
        compiler_params=pltpu.CompilerParams(vmem_limit_bytes=16 * 2**20),
        cost_estimate=pl.CostEstimate(flops=6 * area * HD, bytes_accessed=5 << 20, transcendentals=area),
        name="late",
    )(q, *state, *kvs)


def combine_body(a_ref, b_ref, c_ref, d_ref, video_out, audio_out):
    refs = (a_ref, b_ref, c_ref, d_ref)
    rows = VID + AUD
    auxes = [ref[rows:, :].astype(F32) for ref in refs]
    which = lax.broadcasted_iota(jnp.int32, (2 * AUX, GW), 0)
    table = jnp.zeros((2 * AUX, GW), F32)
    for h in range(HPG):
        lses = [x[3 * h : 3 * h + 1] + x[3 * h + 1 : 3 * h + 2] + x[3 * h + 2 : 3 * h + 3] for x in auxes]
        top = functools.reduce(jnp.maximum, lses)
        weights = [jnp.exp2(x - top) for x in lses]
        scale = 1.0 / sum(weights)
        for i, w in enumerate(weights):
            w = w * scale
            hi = w.astype(BF16).astype(F32)
            at = 2 * (NX * h + i)
            table = jnp.where(which == at, hi, jnp.where(which == at + 1, w - hi, table))
    table = table.astype(BF16)
    which = lax.broadcasted_iota(jnp.int32, (2 * AUX, HD), 0)
    for h in range(HPG):
        cols = slice(h * HD, (h + 1) * HD)
        out = 0.0
        for i, ref in enumerate(refs):
            at = 2 * (NX * h + i)
            pick = jnp.where((which == at) | (which == at + 1), 1.0, 0.0).astype(BF16)
            out = out + ref[0:rows, cols].astype(F32) * dot_tn(table, pick)[0:rows]
        out = out.astype(BF16)
        for g in range(NZ):
            video_out[g, :, cols] = out[g * TOK : (g + 1) * TOK]
        audio_out[:, cols] = out[VID:]


def combine(parts):
    return pl.pallas_call(
        combine_body,
        out_shape=(
            jax.ShapeDtypeStruct((NZ, TOK, GW), BF16),
            jax.ShapeDtypeStruct((AUD, GW), BF16),
        ),
        in_specs=[VMEM] * NX,
        out_specs=(VMEM, VMEM),
        compiler_params=SMALL,
        name="combine",
    )(*parts)


def spread_body(video_ref, audio_ref, video_out, audio_out, rows_ref, sems):
    audio_copy = pltpu.make_async_copy(audio_ref, audio_out, sems.at[0])
    audio_copy.start()
    for g in range(NZ):
        rows_ref[:, g * GW : (g + 1) * GW] = video_ref[g]
    video_copy = pltpu.make_async_copy(rows_ref, video_out, sems.at[1])
    video_copy.start()
    audio_copy.wait()
    video_copy.wait()


def spread(video, audio):
    return pl.pallas_call(
        spread_body,
        out_shape=(
            jax.ShapeDtypeStruct((TOK, NZ * GW), BF16),
            jax.ShapeDtypeStruct((AUD, GW), BF16),
        ),
        in_specs=[VMEM, VMEM],
        out_specs=(ANY, ANY),
        scratch_shapes=[pltpu.VMEM((TOK, NZ * GW), BF16), pltpu.SemaphoreType.DMA((2,))],
        compiler_params=SMALL,
        name="spread",
    )(video, audio)


def shift(x, axis, n, k):
    return lax.ppermute(x, axis, [(i, (i + k) % n) for i in range(n)])


PLACES = ((2, 1), (1, 1), (2, 0), (1, 0), (0, 0), (3, 0), (0, 1), (3, 1))


def audio_pairs():
    pairs = []
    for group in range(NZ):
        for ahead, (dx, dy) in enumerate(PLACES):
            there = ((group // 2 + dx) % NX) * 2 + (group % 2 + dy) % 2
            pairs.append((group * NZ + (group + ahead) % NZ, there * NZ + group))
    return pairs


def audio_z():
    group = lax.axis_index("z")
    dx = lax.rem(lax.axis_index("x") + NX - group // 2, NX)
    dy = lax.rem(lax.axis_index("yh") + 2 - lax.rem(group, 2), 2)
    ahead = 0
    for n, (px, py) in enumerate(PLACES):
        ahead = jnp.where((dx == px) & (dy == py), n, ahead)
    return lax.rem(group + ahead, NZ)


def to_group(x):
    return lax.ppermute(x, ("x", "yh", "z"), audio_pairs())


def from_group(x):
    return lax.ppermute(x, ("x", "yh", "z"), [(b, a) for a, b in audio_pairs()])


def on_device(video_q, video_k, video_v, audio_q, audio_k, audio_v, align):
    aud = to_group(jnp.concatenate([audio_q, audio_k, audio_v], axis=1))
    got = lax.all_to_all(
        pack(align, video_q, video_k, video_v), "z", split_axis=0, concat_axis=0, tiled=True
    )
    q_own, kv_own = join(got, aud)
    y = ("yh", "yl")
    core = functools.partial(shift, axis="c", n=NC, k=1)
    right, left = [shift(kv_own, y, NY, k) for k in (1, 3)]
    q_right, q_left = [shift(q_own, "x", NX, k) for k in (1, 3)]
    q_far = shift(q_right, "x", NX, 1)
    got = lax.optimization_barrier([left, right, q_left, q_right, q_own, kv_own])
    left, right, q_left, q_right, q_own, kv_own = got
    far = [shift(right[0:VID], y, NY, 1), shift(left[VID:], y, NY, 3)]
    kvs = [kv_own, right, left] + [core(b) for b in (kv_own, right, left)]
    state = early([q_right, q_left, q_own], kvs)
    far, q_far, state = lax.optimization_barrier((far, q_far, state))
    others = [core(b) for b in far]
    state_far = early([q_far], kvs)
    kvs = kvs + far + others
    part_far, state = lax.optimization_barrier((late(q_far, state_far, kvs), state))
    parts = [part_far] + [late(q, state[2 * i : 2 * i + 2], kvs) for i, q in enumerate([q_right, q_left, q_own])]
    back = [shift(p, "x", NX, -k) for p, k in zip(parts, (2, 1, 3))]
    video, audio = combine(parts[3:] + back)
    video = lax.all_to_all(video, "z", split_axis=0, concat_axis=0, tiled=True)
    return spread(video, from_group(audio))


def solution(mesh):
    grid = Mesh(np.asarray(mesh.devices).reshape(4, 2, 2, 8, 2), ("x", "yh", "yl", "z", "c"))
    seq, head = ("yl", "z", "c"), ("x", "yh")
    rows = P(seq + head, None)
    audio = P(seq, head)
    return jax.shard_map(
        on_device,
        mesh=grid,
        in_specs=(rows, rows, rows, audio, audio, audio, P(seq + head)),
        out_specs=(rows, audio),
        check_vma=False,
    )
```

```python
import functools

import jax
import jax.numpy as jnp
import numpy as np
from jax import lax
from jax.experimental import pallas as pl
from jax.experimental.pallas import tpu as pltpu
from jax.sharding import Mesh
from jax.sharding import PartitionSpec as P

HD = 128
HPG = 3
GW = HPG * HD
NZ, NX, NY, NC = 8, 4, 4, 2
TOK = 32
AUD = 16
VID = NZ * TOK
STAMPS = 8
AUX = 16
QROWS = VID + AUD + AUX
KROWS = 2 * VID + 2 * AUD + AUX
NKB = NY * NC
EARLY = 6
WIN = 64.0
NEG = -1e30
C2 = HD**-0.5 * 1.4426950408889634
F32, BF16 = jnp.float32, jnp.bfloat16
VMEM = pl.BlockSpec(memory_space=pltpu.VMEM)
SMEM = pl.BlockSpec(memory_space=pltpu.SMEM)
ANY = pl.BlockSpec(memory_space=pl.ANY)
SMALL = pltpu.CompilerParams(vmem_limit_bytes=6 * 2**20)


def pack_body(align_ref, q_ref, k_ref, v_ref, out):
    first = lax.axis_index("z") * TOK
    lane = lax.broadcasted_iota(jnp.int32, (1, GW), 1)
    row = jnp.zeros((1, GW), jnp.int32)
    for i in range(TOK):
        row = jnp.where(lane == first + i, align_ref[i], row)
    high = (row >> 4).astype(F32)
    low = (row & 15).astype(F32)
    which = lax.broadcasted_iota(jnp.int32, (STAMPS, HD), 0)
    stamps = jnp.zeros((STAMPS, HD), F32)
    for n, part in enumerate((high[:, 0:HD], high[:, HD:VID], low[:, 0:HD], low[:, HD:VID])):
        stamps = jnp.where(which == n, part, stamps)
    stamps = stamps.astype(BF16)
    for g in range(NZ):
        for n, ref in enumerate((q_ref, k_ref, v_ref)):
            for h in range(HPG):
                at = (n * HPG + h) * TOK
                out[g, at : at + TOK, :] = ref[:, (g * HPG + h) * HD : (g * HPG + h + 1) * HD]
        out[g, 3 * HPG * TOK :, :] = stamps


def pack(align, q, k, v):
    return pl.pallas_call(
        pack_body,
        out_shape=jax.ShapeDtypeStruct((NZ, 3 * HPG * TOK + STAMPS, HD), BF16),
        in_specs=[SMEM, VMEM, VMEM, VMEM],
        out_specs=VMEM,
        name="pack",
    )(align, q, k, v)


def audio_times(start):
    lane = lax.broadcasted_iota(jnp.int32, (AUX, GW), 1) - VID
    which = lax.broadcasted_iota(jnp.int32, (AUX, GW), 0)
    stamp = lane + start
    here = (lane >= 0) & (lane < AUD)
    part = jnp.where(which == 0, stamp >> 4, jnp.where(which == 1, stamp & 15, 0))
    return jnp.where(here, part, 0).astype(F32)


def join_body(got_ref, aud_ref, q_out, kv_out):
    block = lax.axis_index("yl") * 16 + audio_z() * 2 + lax.axis_index("c")
    stamps = jnp.zeros((STAMPS, HD), F32)
    for g in range(NZ):
        for h in range(HPG):
            cols = slice(h * HD, (h + 1) * HD)
            for n, (out, first) in enumerate(((q_out, 0), (kv_out, 0), (kv_out, VID))):
                at = (n * HPG + h) * TOK
                out[first + g * TOK : first + (g + 1) * TOK, cols] = got_ref[g, at : at + TOK, :]
        stamps = stamps + got_ref[g, 3 * HPG * TOK :, :].astype(F32)
    none = jnp.zeros((1, HD), F32)
    high = jnp.concatenate([stamps[0:1], stamps[1:2], none], axis=1)
    low = jnp.concatenate([stamps[2:3], stamps[3:4], none], axis=1)
    which = lax.broadcasted_iota(jnp.int32, (AUX, GW), 0)
    aux = jnp.where(which == 0, high, jnp.where(which == 1, low, 0.0)) + audio_times(block * AUD)
    aux = aux.astype(BF16)
    q_out[VID : VID + AUD, :] = aud_ref[:, 0:GW]
    kv_out[2 * VID : 2 * VID + AUD, :] = aud_ref[:, GW : 2 * GW]
    kv_out[2 * VID + AUD : 2 * VID + 2 * AUD, :] = aud_ref[:, 2 * GW :]
    q_out[VID + AUD :, :] = aux
    kv_out[2 * VID + 2 * AUD :, :] = aux


def join(got, aud):
    return pl.pallas_call(
        join_body,
        out_shape=(
            pltpu.VMEM((QROWS, GW), BF16),
            pltpu.VMEM((KROWS, GW), BF16),
        ),
        in_specs=[VMEM, VMEM],
        out_specs=(VMEM, VMEM),
        compiler_params=SMALL,
        name="join",
    )(got, aud)


def place(rows):
    return sum(
        pltpu.roll(jnp.broadcast_to(row, (8, HD)), i * AUD, 1) if i else jnp.broadcast_to(row, (8, HD))
        for i, row in enumerate(rows)
    )[0:1, :]


def dot_nt(a, b):
    return lax.dot_general(a, b, (((1,), (1,)), ((), ())), preferred_element_type=F32)


def dot_tn(a, b):
    return lax.dot_general(a, b, (((0,), (0,)), ((), ())), preferred_element_type=F32)


def times_of(ref, first):
    aux = ref[first : first + AUX, :].astype(F32)
    return aux[0:1, :] * 16.0 + aux[1:2, :]


def column_times(q_ref):
    which = lax.broadcasted_iota(jnp.int32, (AUX, HD), 0)
    pick = jnp.where(which == 0, 16.0, jnp.where(which == 1, 1.0, 0.0)).astype(BF16)
    return dot_tn(q_ref[VID + AUD : QROWS, :], pick)


def side_by_side(x):
    return jnp.concatenate([x, x], axis=1)


def scores(q, k_refs, cols, near_audio, s_ref, h):
    top = None
    for j, k_ref in enumerate(k_refs):
        s = dot_nt(q, k_ref[0:VID, cols])
        s = jnp.concatenate([s[0:VID], jnp.where(near_audio[j], s[VID:], NEG)], axis=0)
        s_ref[h, :, j * VID : (j + 1) * VID] = s
        part = jnp.maximum(s[:, 0:HD], s[:, HD:])
        top = part if top is None else jnp.maximum(top, part)
    return top


def weigh(s, top, v, ones):
    p = jnp.exp2((s - top) * C2).astype(BF16)
    v = jnp.concatenate([v, ones[0 : v.shape[0]]], axis=1)
    return jnp.dot(p, v, preferred_element_type=F32)


def early_body(*refs):
    n = (len(refs) - EARLY - 1) // 3
    q_refs, k_refs = refs[0:n], refs[n : n + EARLY]
    outs, s_ref = refs[n + EARLY : -1], refs[-1]
    k_times = [times_of(k_ref, 2 * VID + 2 * AUD) for k_ref in k_refs]
    ones = jnp.ones((VID, HD), BF16)

    def start(i, h):
        q_ref = q_refs[i]
        cols = slice(h * HD, (h + 1) * HD)
        column = side_by_side(column_times(q_ref)[VID : VID + AUD])
        near_audio = [jnp.abs(column - t[:, 0:VID]) <= WIN for t in k_times]
        top = scores(q_ref[0 : VID + AUD, cols], k_refs, cols, near_audio, s_ref, (i * HPG + h) % 3)
        return jnp.max(top, axis=1, keepdims=True)

    def end(i, h, top):
        cols = slice(h * HD, (h + 1) * HD)
        acc = 0.0
        for j, k_ref in enumerate(k_refs):
            s = s_ref[(i * HPG + h) % 3, :, j * VID : (j + 1) * VID]
            acc = acc + weigh(s, top, k_ref[VID : 2 * VID, cols], ones)
        total = acc[:, HD:]
        outs[2 * i][:, cols] = acc[:, 0:HD] / total
        outs[2 * i + 1][:, cols] = top * C2 + jnp.log2(total)

    work = [(i, h) for i in range(n) for h in range(HPG)]
    tops = {}
    for m, item in enumerate(work):
        tops[item] = start(*item)
        if m >= 2:
            end(*work[m - 2], tops[work[m - 2]])
    for item in work[-2:]:
        end(*item, tops[item])


def early(qs, kvs):
    n, rows, nk = len(qs), VID + AUD, EARLY * VID
    area = n * rows * nk * HPG
    return pl.pallas_call(
        early_body,
        out_shape=tuple(jax.ShapeDtypeStruct((rows, GW), F32) for _ in range(2 * n)),
        in_specs=[VMEM] * (n + EARLY),
        out_specs=tuple(VMEM for _ in range(2 * n)),
        scratch_shapes=[pltpu.VMEM((3, rows, nk), F32)],
        compiler_params=pltpu.CompilerParams(vmem_limit_bytes=16 * 2**20),
        cost_estimate=pl.CostEstimate(flops=6 * area * HD, bytes_accessed=4 << 20, transcendentals=area),
        name="early",
    )(*qs, *kvs)


class Block:
    def __init__(self, keys, rest):
        self.keys, self.rest = keys, rest

    def __getitem__(self, at):
        rows, cols = at
        if rows.stop <= VID:
            return self.keys[rows, cols]
        return self.rest[rows.start - VID : rows.stop - VID, cols]


def late_body(q_ref, o_ref, l_ref, *refs):
    out, s_ref = refs[EARLY + 4 :]
    rows = VID + AUD
    rest = (Block(*refs[EARLY : EARLY + 2]), Block(*refs[EARLY + 2 : EARLY + 4]))
    k_refs = refs[0:EARLY] + rest
    ka_times = place([times_of(k_ref, 2 * VID + 2 * AUD)[:, VID:] for k_ref in k_refs])
    k_times = [times_of(k_ref, 2 * VID + 2 * AUD) for k_ref in rest]
    column = column_times(q_ref)
    near_video = jnp.abs(column[0:VID] - ka_times) <= WIN
    column = side_by_side(column[VID:rows])
    near_audio = [jnp.abs(column - t[:, 0:VID]) <= WIN for t in k_times]
    ones = jnp.ones((VID, HD), BF16)
    eye = lax.broadcasted_iota(jnp.int32, (HD, HD), 0) == lax.broadcasted_iota(jnp.int32, (HD, HD), 1)
    which = lax.broadcasted_iota(jnp.int32, (AUX, GW), 0)
    first = len(rest) * VID

    def start(h):
        cols = slice(h * HD, (h + 1) * HD)
        q = q_ref[0:rows, cols]
        top = scores(q, rest, cols, near_audio, s_ref, h)
        s = dot_nt(q, jnp.concatenate([k[2 * VID : 2 * VID + AUD, cols] for k in k_refs], axis=0))
        s = jnp.concatenate([jnp.where(near_video, s[0:VID], NEG), s[VID:]], axis=0)
        s_ref[h, :, first:] = s
        return jnp.max(jnp.maximum(top, s), axis=1, keepdims=True)

    def end(h, top):
        cols = slice(h * HD, (h + 1) * HD)
        at = 2 * VID + AUD
        acc = weigh(s_ref[h, :, first:], top, jnp.concatenate([k[at : at + AUD, cols] for k in k_refs], axis=0), ones)
        for j, k_ref in enumerate(rest):
            acc = acc + weigh(s_ref[h, :, j * VID : (j + 1) * VID], top, k_ref[VID : 2 * VID, cols], ones)
        base = top * C2
        before = l_ref[:, cols]
        most = jnp.maximum(base, before)
        w_here, w_before = jnp.exp2(base - most), jnp.exp2(before - most)
        total = acc[:, HD:] * w_here + w_before
        out[0:rows, cols] = ((acc[:, 0:HD] * w_here + o_ref[:, cols] * w_before) / total).astype(BF16)
        lse = most + jnp.log2(total)
        row = jnp.concatenate(
            [
                jnp.sum(jnp.where(eye[0:n], lse[a : a + n], 0.0), axis=0, keepdims=True)
                for a, n in ((0, HD), (HD, HD), (VID, AUD))
            ],
            axis=1,
        )
        hi = row.astype(BF16).astype(F32)
        mid = (row - hi).astype(BF16).astype(F32)
        low = row - hi - mid
        return jnp.where(which == 3 * h, hi, jnp.where(which == 3 * h + 1, mid, jnp.where(which == 3 * h + 2, low, 0.0)))

    tops = [start(h) for h in range(HPG)]
    out[rows:, :] = sum(end(h, tops[h]) for h in range(HPG)).astype(BF16)


def late(q, state, kvs):
    rows, nk = VID + AUD, (NKB - EARLY) * VID + NKB * AUD
    area = rows * nk * HPG
    return pl.pallas_call(
        late_body,
        out_shape=jax.ShapeDtypeStruct((QROWS, GW), BF16),
        in_specs=[VMEM] * (3 + EARLY + 4),
        out_specs=VMEM,
        scratch_shapes=[pltpu.VMEM((HPG, rows, nk), F32)],
        compiler_params=pltpu.CompilerParams(vmem_limit_bytes=16 * 2**20),
        cost_estimate=pl.CostEstimate(flops=6 * area * HD, bytes_accessed=5 << 20, transcendentals=area),
        name="late",
    )(q, *state, *kvs)


def combine_body(a_ref, b_ref, c_ref, d_ref, video_out, audio_out):
    refs = (a_ref, b_ref, c_ref, d_ref)
    rows = VID + AUD
    auxes = [ref[rows:, :].astype(F32) for ref in refs]
    which = lax.broadcasted_iota(jnp.int32, (2 * AUX, GW), 0)
    table = jnp.zeros((2 * AUX, GW), F32)
    for h in range(HPG):
        lses = [x[3 * h : 3 * h + 1] + x[3 * h + 1 : 3 * h + 2] + x[3 * h + 2 : 3 * h + 3] for x in auxes]
        top = functools.reduce(jnp.maximum, lses)
        weights = [jnp.exp2(x - top) for x in lses]
        scale = 1.0 / sum(weights)
        for i, w in enumerate(weights):
            w = w * scale
            hi = w.astype(BF16).astype(F32)
            at = 2 * (NX * h + i)
            table = jnp.where(which == at, hi, jnp.where(which == at + 1, w - hi, table))
    table = table.astype(BF16)
    which = lax.broadcasted_iota(jnp.int32, (2 * AUX, HD), 0)
    for h in range(HPG):
        cols = slice(h * HD, (h + 1) * HD)
        out = 0.0
        for i, ref in enumerate(refs):
            at = 2 * (NX * h + i)
            pick = jnp.where((which == at) | (which == at + 1), 1.0, 0.0).astype(BF16)
            out = out + ref[0:rows, cols].astype(F32) * dot_tn(table, pick)[0:rows]
        out = out.astype(BF16)
        for g in range(NZ):
            video_out[g, :, cols] = out[g * TOK : (g + 1) * TOK]
        audio_out[:, cols] = out[VID:]


def combine(parts):
    return pl.pallas_call(
        combine_body,
        out_shape=(
            jax.ShapeDtypeStruct((NZ, TOK, GW), BF16),
            jax.ShapeDtypeStruct((AUD, GW), BF16),
        ),
        in_specs=[VMEM] * NX,
        out_specs=(VMEM, VMEM),
        compiler_params=SMALL,
        name="combine",
    )(*parts)


def spread_body(video_ref, audio_ref, video_out, audio_out, rows_ref, sems):
    audio_copy = pltpu.make_async_copy(audio_ref, audio_out, sems.at[0])
    audio_copy.start()
    for g in range(NZ):
        rows_ref[:, g * GW : (g + 1) * GW] = video_ref[g]
    video_copy = pltpu.make_async_copy(rows_ref, video_out, sems.at[1])
    video_copy.start()
    audio_copy.wait()
    video_copy.wait()


def spread(video, audio):
    return pl.pallas_call(
        spread_body,
        out_shape=(
            jax.ShapeDtypeStruct((TOK, NZ * GW), BF16),
            jax.ShapeDtypeStruct((AUD, GW), BF16),
        ),
        in_specs=[VMEM, VMEM],
        out_specs=(ANY, ANY),
        scratch_shapes=[pltpu.VMEM((TOK, NZ * GW), BF16), pltpu.SemaphoreType.DMA((2,))],
        compiler_params=SMALL,
        name="spread",
    )(video, audio)


def shift(x, axis, n, k):
    return lax.ppermute(x, axis, [(i, (i + k) % n) for i in range(n)])


PLACES = ((2, 1), (1, 1), (2, 0), (1, 0), (0, 0), (3, 0), (0, 1), (3, 1))


def audio_pairs():
    pairs = []
    for group in range(NZ):
        for ahead, (dx, dy) in enumerate(PLACES):
            there = ((group // 2 + dx) % NX) * 2 + (group % 2 + dy) % 2
            pairs.append((group * NZ + (group + ahead) % NZ, there * NZ + group))
    return pairs


def audio_z():
    group = lax.axis_index("z")
    dx = lax.rem(lax.axis_index("x") + NX - group // 2, NX)
    dy = lax.rem(lax.axis_index("yh") + 2 - lax.rem(group, 2), 2)
    ahead = 0
    for n, (px, py) in enumerate(PLACES):
        ahead = jnp.where((dx == px) & (dy == py), n, ahead)
    return lax.rem(group + ahead, NZ)


def to_group(x):
    return lax.ppermute(x, ("x", "yh", "z"), audio_pairs())


def from_group(x):
    return lax.ppermute(x, ("x", "yh", "z"), [(b, a) for a, b in audio_pairs()])


def on_device(video_q, video_k, video_v, audio_q, audio_k, audio_v, align):
    aud = to_group(jnp.concatenate([audio_q, audio_k, audio_v], axis=1))
    got = lax.all_to_all(
        pack(align, video_q, video_k, video_v), "z", split_axis=0, concat_axis=0, tiled=True
    )
    q_own, kv_own = join(got, aud)
    y = ("yh", "yl")
    core = functools.partial(shift, axis="c", n=NC, k=1)
    right, left = [shift(kv_own, "x", NX, k) for k in (1, 3)]
    q_right, q_left = [shift(q_own, y, NY, k) for k in (1, 3)]
    q_far = shift(q_right, y, NY, 1)
    got = lax.optimization_barrier([left, right, q_left, q_right, q_own, kv_own])
    left, right, q_left, q_right, q_own, kv_own = got
    far = [shift(right[0:VID], "x", NX, 1), shift(left[VID:], "x", NX, 3)]
    kvs = [kv_own, right, left] + [core(b) for b in (kv_own, right, left)]
    state = early([q_right, q_left, q_own], kvs)
    far, q_far, state = lax.optimization_barrier((far, q_far, state))
    others = [core(b) for b in far]
    state_far = early([q_far], kvs)
    kvs = kvs + far + others
    part_far, state = lax.optimization_barrier((late(q_far, state_far, kvs), state))
    parts = [part_far] + [late(q, state[2 * i : 2 * i + 2], kvs) for i, q in enumerate([q_right, q_left, q_own])]
    back = [shift(p, y, NY, -k) for p, k in zip(parts, (2, 1, 3))]
    video, audio = combine(parts[3:] + back)
    video = lax.all_to_all(video, "z", split_axis=0, concat_axis=0, tiled=True)
    return spread(video, from_group(audio))


def solution(mesh):
    grid = Mesh(np.asarray(mesh.devices).reshape(4, 2, 2, 8, 2), ("x", "yh", "yl", "z", "c"))
    seq, head = ("yl", "z", "c"), ("x", "yh")
    rows = P(seq + head, None)
    audio = P(seq, head)
    return jax.shard_map(
        on_device,
        mesh=grid,
        in_specs=(rows, rows, rows, audio, audio, audio, P(seq + head)),
        out_specs=(rows, audio),
        check_vma=False,
    )
```

```python
import functools

import jax
import jax.numpy as jnp
import numpy as np
from jax import lax
from jax.experimental import pallas as pl
from jax.experimental.pallas import tpu as pltpu
from jax.sharding import Mesh
from jax.sharding import PartitionSpec as P

HD = 128
HPG = 3
GW = HPG * HD
NZ, NX, NY, NC = 8, 4, 4, 2
TOK = 32
AUD = 16
VID = NZ * TOK
STAMPS = 8
AUX = 16
QROWS = VID + AUD + AUX
KROWS = 2 * VID + 2 * AUD + AUX
NKB = NY * NC
EARLY = 6
WIN = 64.0
NEG = -1e30
C2 = HD**-0.5 * 1.4426950408889634
F32, BF16 = jnp.float32, jnp.bfloat16
VMEM = pl.BlockSpec(memory_space=pltpu.VMEM)
SMEM = pl.BlockSpec(memory_space=pltpu.SMEM)
ANY = pl.BlockSpec(memory_space=pl.ANY)
SMALL = pltpu.CompilerParams(vmem_limit_bytes=6 * 2**20)


def pack_body(align_ref, q_ref, k_ref, v_ref, out):
    first = lax.axis_index("z") * TOK
    lane = lax.broadcasted_iota(jnp.int32, (1, GW), 1)
    row = jnp.zeros((1, GW), jnp.int32)
    for i in range(TOK):
        row = jnp.where(lane == first + i, align_ref[i], row)
    high = (row >> 4).astype(F32)
    low = (row & 15).astype(F32)
    which = lax.broadcasted_iota(jnp.int32, (STAMPS, HD), 0)
    stamps = jnp.zeros((STAMPS, HD), F32)
    for n, part in enumerate((high[:, 0:HD], high[:, HD:VID], low[:, 0:HD], low[:, HD:VID])):
        stamps = jnp.where(which == n, part, stamps)
    stamps = stamps.astype(BF16)
    for g in range(NZ):
        for n, ref in enumerate((q_ref, k_ref, v_ref)):
            for h in range(HPG):
                at = (n * HPG + h) * TOK
                out[g, at : at + TOK, :] = ref[:, (g * HPG + h) * HD : (g * HPG + h + 1) * HD]
        out[g, 3 * HPG * TOK :, :] = stamps


def pack(align, q, k, v):
    return pl.pallas_call(
        pack_body,
        out_shape=jax.ShapeDtypeStruct((NZ, 3 * HPG * TOK + STAMPS, HD), BF16),
        in_specs=[SMEM, VMEM, VMEM, VMEM],
        out_specs=VMEM,
        name="pack",
    )(align, q, k, v)


def audio_times(start):
    lane = lax.broadcasted_iota(jnp.int32, (AUX, GW), 1) - VID
    which = lax.broadcasted_iota(jnp.int32, (AUX, GW), 0)
    stamp = lane + start
    here = (lane >= 0) & (lane < AUD)
    part = jnp.where(which == 0, stamp >> 4, jnp.where(which == 1, stamp & 15, 0))
    return jnp.where(here, part, 0).astype(F32)


def join_body(got_ref, aud_ref, q_out, kv_out):
    block = lax.axis_index("yl") * 16 + audio_z() * 2 + lax.axis_index("c")
    stamps = jnp.zeros((STAMPS, HD), F32)
    for g in range(NZ):
        for h in range(HPG):
            cols = slice(h * HD, (h + 1) * HD)
            for n, (out, first) in enumerate(((q_out, 0), (kv_out, 0), (kv_out, VID))):
                at = (n * HPG + h) * TOK
                out[first + g * TOK : first + (g + 1) * TOK, cols] = got_ref[g, at : at + TOK, :]
        stamps = stamps + got_ref[g, 3 * HPG * TOK :, :].astype(F32)
    none = jnp.zeros((1, HD), F32)
    high = jnp.concatenate([stamps[0:1], stamps[1:2], none], axis=1)
    low = jnp.concatenate([stamps[2:3], stamps[3:4], none], axis=1)
    which = lax.broadcasted_iota(jnp.int32, (AUX, GW), 0)
    aux = jnp.where(which == 0, high, jnp.where(which == 1, low, 0.0)) + audio_times(block * AUD)
    aux = aux.astype(BF16)
    q_out[VID : VID + AUD, :] = aud_ref[:, 0:GW]
    kv_out[2 * VID : 2 * VID + AUD, :] = aud_ref[:, GW : 2 * GW]
    kv_out[2 * VID + AUD : 2 * VID + 2 * AUD, :] = aud_ref[:, 2 * GW :]
    q_out[VID + AUD :, :] = aux
    kv_out[2 * VID + 2 * AUD :, :] = aux


def join(got, aud):
    return pl.pallas_call(
        join_body,
        out_shape=(
            pltpu.VMEM((QROWS, GW), BF16),
            pltpu.VMEM((KROWS, GW), BF16),
        ),
        in_specs=[VMEM, VMEM],
        out_specs=(VMEM, VMEM),
        compiler_params=SMALL,
        name="join",
    )(got, aud)


def place(rows):
    return sum(
        pltpu.roll(jnp.broadcast_to(row, (8, HD)), i * AUD, 1) if i else jnp.broadcast_to(row, (8, HD))
        for i, row in enumerate(rows)
    )[0:1, :]


def dot_nt(a, b):
    return lax.dot_general(a, b, (((1,), (1,)), ((), ())), preferred_element_type=F32)


def dot_tn(a, b):
    return lax.dot_general(a, b, (((0,), (0,)), ((), ())), preferred_element_type=F32)


def times_of(ref, first):
    aux = ref[first : first + AUX, :].astype(F32)
    return aux[0:1, :] * 16.0 + aux[1:2, :]


def column_times(q_ref):
    which = lax.broadcasted_iota(jnp.int32, (AUX, HD), 0)
    pick = jnp.where(which == 0, 16.0, jnp.where(which == 1, 1.0, 0.0)).astype(BF16)
    return dot_tn(q_ref[VID + AUD : QROWS, :], pick)


def side_by_side(x):
    return jnp.concatenate([x, x], axis=1)


def scores(q, k_refs, cols, near_audio, s_ref, h):
    top = None
    for j, k_ref in enumerate(k_refs):
        s = dot_nt(q, k_ref[0:VID, cols])
        s = jnp.concatenate([s[0:VID], jnp.where(near_audio[j], s[VID:], NEG)], axis=0)
        s_ref[h, :, j * VID : (j + 1) * VID] = s
        part = jnp.maximum(s[:, 0:HD], s[:, HD:])
        top = part if top is None else jnp.maximum(top, part)
    return top


def weigh(s, top, v, ones):
    p = jnp.exp2((s - top) * C2).astype(BF16)
    v = jnp.concatenate([v, ones[0 : v.shape[0]]], axis=1)
    return jnp.dot(p, v, preferred_element_type=F32)


def early_body(*refs):
    n = (len(refs) - EARLY - 1) // 3
    q_refs, k_refs = refs[0:n], refs[n : n + EARLY]
    outs, s_ref = refs[n + EARLY : -1], refs[-1]
    k_times = [times_of(k_ref, 2 * VID + 2 * AUD) for k_ref in k_refs]
    ones = jnp.ones((VID, HD), BF16)

    def start(i, h):
        q_ref = q_refs[i]
        cols = slice(h * HD, (h + 1) * HD)
        column = side_by_side(column_times(q_ref)[VID : VID + AUD])
        near_audio = [jnp.abs(column - t[:, 0:VID]) <= WIN for t in k_times]
        top = scores(q_ref[0 : VID + AUD, cols], k_refs, cols, near_audio, s_ref, (i * HPG + h) % 3)
        return jnp.max(top, axis=1, keepdims=True)

    def end(i, h, top):
        cols = slice(h * HD, (h + 1) * HD)
        acc = 0.0
        for j, k_ref in enumerate(k_refs):
            s = s_ref[(i * HPG + h) % 3, :, j * VID : (j + 1) * VID]
            acc = acc + weigh(s, top, k_ref[VID : 2 * VID, cols], ones)
        total = acc[:, HD:]
        outs[2 * i][:, cols] = acc[:, 0:HD] / total
        outs[2 * i + 1][:, cols] = top * C2 + jnp.log2(total)

    work = [(i, h) for i in range(n) for h in range(HPG)]
    tops = {}
    for m, item in enumerate(work):
        tops[item] = start(*item)
        if m >= 2:
            end(*work[m - 2], tops[work[m - 2]])
    for item in work[-2:]:
        end(*item, tops[item])


def early(qs, kvs):
    n, rows, nk = len(qs), VID + AUD, EARLY * VID
    area = n * rows * nk * HPG
    return pl.pallas_call(
        early_body,
        out_shape=tuple(jax.ShapeDtypeStruct((rows, GW), F32) for _ in range(2 * n)),
        in_specs=[VMEM] * (n + EARLY),
        out_specs=tuple(VMEM for _ in range(2 * n)),
        scratch_shapes=[pltpu.VMEM((3, rows, nk), F32)],
        compiler_params=pltpu.CompilerParams(vmem_limit_bytes=16 * 2**20),
        cost_estimate=pl.CostEstimate(flops=6 * area * HD, bytes_accessed=4 << 20, transcendentals=area),
        name="early",
    )(*qs, *kvs)


class Block:
    def __init__(self, keys, rest):
        self.keys, self.rest = keys, rest

    def __getitem__(self, at):
        rows, cols = at
        if rows.stop <= VID:
            return self.keys[rows, cols]
        return self.rest[rows.start - VID : rows.stop - VID, cols]


def late_body(q_ref, o_ref, l_ref, *refs):
    out, s_ref = refs[EARLY + 4 :]
    rows = VID + AUD
    rest = (Block(*refs[EARLY : EARLY + 2]), Block(*refs[EARLY + 2 : EARLY + 4]))
    k_refs = refs[0:EARLY] + rest
    ka_times = place([times_of(k_ref, 2 * VID + 2 * AUD)[:, VID:] for k_ref in k_refs])
    k_times = [times_of(k_ref, 2 * VID + 2 * AUD) for k_ref in rest]
    column = column_times(q_ref)
    near_video = jnp.abs(column[0:VID] - ka_times) <= WIN
    column = side_by_side(column[VID:rows])
    near_audio = [jnp.abs(column - t[:, 0:VID]) <= WIN for t in k_times]
    ones = jnp.ones((VID, HD), BF16)
    eye = lax.broadcasted_iota(jnp.int32, (HD, HD), 0) == lax.broadcasted_iota(jnp.int32, (HD, HD), 1)
    which = lax.broadcasted_iota(jnp.int32, (AUX, GW), 0)
    first = len(rest) * VID

    def start(h):
        cols = slice(h * HD, (h + 1) * HD)
        q = q_ref[0:rows, cols]
        top = scores(q, rest, cols, near_audio, s_ref, h)
        s = dot_nt(q, jnp.concatenate([k[2 * VID : 2 * VID + AUD, cols] for k in k_refs], axis=0))
        s = jnp.concatenate([jnp.where(near_video, s[0:VID], NEG), s[VID:]], axis=0)
        s_ref[h, :, first:] = s
        return jnp.max(jnp.maximum(top, s), axis=1, keepdims=True)

    def end(h, top):
        cols = slice(h * HD, (h + 1) * HD)
        at = 2 * VID + AUD
        acc = weigh(s_ref[h, :, first:], top, jnp.concatenate([k[at : at + AUD, cols] for k in k_refs], axis=0), ones)
        for j, k_ref in enumerate(rest):
            acc = acc + weigh(s_ref[h, :, j * VID : (j + 1) * VID], top, k_ref[VID : 2 * VID, cols], ones)
        base = top * C2
        before = l_ref[:, cols]
        most = jnp.maximum(base, before)
        w_here, w_before = jnp.exp2(base - most), jnp.exp2(before - most)
        total = acc[:, HD:] * w_here + w_before
        out[0:rows, cols] = ((acc[:, 0:HD] * w_here + o_ref[:, cols] * w_before) / total).astype(BF16)
        lse = most + jnp.log2(total)
        row = jnp.concatenate(
            [
                jnp.sum(jnp.where(eye[0:n], lse[a : a + n], 0.0), axis=0, keepdims=True)
                for a, n in ((0, HD), (HD, HD), (VID, AUD))
            ],
            axis=1,
        )
        hi = row.astype(BF16).astype(F32)
        mid = (row - hi).astype(BF16).astype(F32)
        low = row - hi - mid
        return jnp.where(which == 3 * h, hi, jnp.where(which == 3 * h + 1, mid, jnp.where(which == 3 * h + 2, low, 0.0)))

    tops = [start(h) for h in range(HPG)]
    out[rows:, :] = sum(end(h, tops[h]) for h in range(HPG)).astype(BF16)


def late(q, state, kvs):
    rows, nk = VID + AUD, (NKB - EARLY) * VID + NKB * AUD
    area = rows * nk * HPG
    return pl.pallas_call(
        late_body,
        out_shape=jax.ShapeDtypeStruct((QROWS, GW), BF16),
        in_specs=[VMEM] * (3 + EARLY + 4),
        out_specs=VMEM,
        scratch_shapes=[pltpu.VMEM((HPG, rows, nk), F32)],
        compiler_params=pltpu.CompilerParams(vmem_limit_bytes=16 * 2**20),
        cost_estimate=pl.CostEstimate(flops=6 * area * HD, bytes_accessed=5 << 20, transcendentals=area),
        name="late",
    )(q, *state, *kvs)


def combine_body(a_ref, b_ref, c_ref, d_ref, video_out, audio_out):
    refs = (a_ref, b_ref, c_ref, d_ref)
    rows = VID + AUD
    auxes = [ref[rows:, :].astype(F32) for ref in refs]
    which = lax.broadcasted_iota(jnp.int32, (2 * AUX, GW), 0)
    table = jnp.zeros((2 * AUX, GW), F32)
    for h in range(HPG):
        lses = [x[3 * h : 3 * h + 1] + x[3 * h + 1 : 3 * h + 2] + x[3 * h + 2 : 3 * h + 3] for x in auxes]
        top = functools.reduce(jnp.maximum, lses)
        weights = [jnp.exp2(x - top) for x in lses]
        scale = 1.0 / sum(weights)
        for i, w in enumerate(weights):
            w = w * scale
            hi = w.astype(BF16).astype(F32)
            at = 2 * (NX * h + i)
            table = jnp.where(which == at, hi, jnp.where(which == at + 1, w - hi, table))
    table = table.astype(BF16)
    which = lax.broadcasted_iota(jnp.int32, (2 * AUX, HD), 0)
    for h in range(HPG):
        cols = slice(h * HD, (h + 1) * HD)
        out = 0.0
        for i, ref in enumerate(refs):
            at = 2 * (NX * h + i)
            pick = jnp.where((which == at) | (which == at + 1), 1.0, 0.0).astype(BF16)
            out = out + ref[0:rows, cols].astype(F32) * dot_tn(table, pick)[0:rows]
        out = out.astype(BF16)
        for g in range(NZ):
            video_out[g, :, cols] = out[g * TOK : (g + 1) * TOK]
        audio_out[:, cols] = out[VID:]


def combine(parts):
    return pl.pallas_call(
        combine_body,
        out_shape=(
            jax.ShapeDtypeStruct((NZ, TOK, GW), BF16),
            jax.ShapeDtypeStruct((AUD, GW), BF16),
        ),
        in_specs=[VMEM] * NX,
        out_specs=(VMEM, VMEM),
        compiler_params=SMALL,
        name="combine",
    )(*parts)


def spread_body(video_ref, audio_ref, video_out, audio_out, rows_ref, sems):
    audio_copy = pltpu.make_async_copy(audio_ref, audio_out, sems.at[0])
    audio_copy.start()
    for g in range(NZ):
        rows_ref[:, g * GW : (g + 1) * GW] = video_ref[g]
    video_copy = pltpu.make_async_copy(rows_ref, video_out, sems.at[1])
    video_copy.start()
    audio_copy.wait()
    video_copy.wait()


def spread(video, audio):
    return pl.pallas_call(
        spread_body,
        out_shape=(
            jax.ShapeDtypeStruct((TOK, NZ * GW), BF16),
            jax.ShapeDtypeStruct((AUD, GW), BF16),
        ),
        in_specs=[VMEM, VMEM],
        out_specs=(ANY, ANY),
        scratch_shapes=[pltpu.VMEM((TOK, NZ * GW), BF16), pltpu.SemaphoreType.DMA((2,))],
        compiler_params=SMALL,
        name="spread",
    )(video, audio)


def shift(x, axis, n, k):
    return lax.ppermute(x, axis, [(i, (i + k) % n) for i in range(n)])


PLACES = ((2, 1), (1, 1), (2, 0), (1, 0), (0, 0), (3, 0), (0, 1), (3, 1))


def audio_pairs():
    pairs = []
    for group in range(NZ):
        for ahead, (dx, dy) in enumerate(PLACES):
            there = ((group // 2 + dx) % NX) * 2 + (group % 2 + dy) % 2
            pairs.append((group * NZ + (group + ahead) % NZ, there * NZ + group))
    return pairs


def audio_z():
    group = lax.axis_index("z")
    dx = lax.rem(lax.axis_index("x") + NX - group // 2, NX)
    dy = lax.rem(lax.axis_index("yh") + 2 - lax.rem(group, 2), 2)
    ahead = 0
    for n, (px, py) in enumerate(PLACES):
        ahead = jnp.where((dx == px) & (dy == py), n, ahead)
    return lax.rem(group + ahead, NZ)


def to_group(x):
    return lax.ppermute(x, ("x", "yh", "z"), audio_pairs())


def from_group(x):
    return lax.ppermute(x, ("x", "yh", "z"), [(b, a) for a, b in audio_pairs()])


def on_device(video_q, video_k, video_v, audio_q, audio_k, audio_v, align):
    aud = to_group(jnp.concatenate([audio_q, audio_k, audio_v], axis=1))
    got = lax.all_to_all(
        pack(align, video_q, video_k, video_v), "z", split_axis=0, concat_axis=0, tiled=True
    )
    q_own, kv_own = join(got, aud)
    y = ("yh", "yl")
    core = functools.partial(shift, axis="c", n=NC, k=1)
    right, left = [shift(kv_own, "x", NX, k) for k in (1, 3)]
    q_right, q_left = [shift(q_own, y, NY, k) for k in (1, 3)]
    q_far = shift(q_right, y, NY, 1)
    other = core(kv_own)
    got = lax.optimization_barrier([left, right, q_left, q_right, q_own, kv_own, other])
    left, right, q_left, q_right, q_own, kv_own, other = got
    far = [shift(right[0:VID], "x", NX, 1), shift(left[VID:], "x", NX, 3)]
    kvs = [kv_own, right, left, other] + [core(b) for b in (right, left)]
    state = early([q_right, q_left, q_own], kvs)
    far, q_far, state = lax.optimization_barrier((far, q_far, state))
    others = [core(b) for b in far]
    state_far = early([q_far], kvs)
    kvs = kvs + far + others
    part_far, state = lax.optimization_barrier((late(q_far, state_far, kvs), state))
    parts = [part_far] + [late(q, state[2 * i : 2 * i + 2], kvs) for i, q in enumerate([q_right, q_left, q_own])]
    back = [shift(p, y, NY, -k) for p, k in zip(parts, (2, 1, 3))]
    video, audio = combine(parts[3:] + back)
    video = lax.all_to_all(video, "z", split_axis=0, concat_axis=0, tiled=True)
    return spread(video, from_group(audio))


def solution(mesh):
    grid = Mesh(np.asarray(mesh.devices).reshape(4, 2, 2, 8, 2), ("x", "yh", "yl", "z", "c"))
    seq, head = ("yl", "z", "c"), ("x", "yh")
    rows = P(seq + head, None)
    audio = P(seq, head)
    return jax.shard_map(
        on_device,
        mesh=grid,
        in_specs=(rows, rows, rows, audio, audio, audio, P(seq + head)),
        out_specs=(rows, audio),
        check_vma=False,
    )
```
